128 devices in a mesh: ch: 4 (over z_lo, core), seq: 32 (over x, z_hi, y).
Axes of the slice: x: 4, y: 4, z: 4 (z_hi: 2, z_lo: 2; z = z_hi * 2 + z_lo), core: 2. Of those that a mesh axis runs over, the one named last changes fastest.
Arguments:
- gate_proj: bfloat16 [12288, 8192], P('seq', 'ch'), may hold values from -120 to 120
- key_proj: bfloat16 [12288, 8192], P('seq', 'ch'), may hold values from -6 to 6
- value_proj: bfloat16 [12288, 8192], P('seq', 'ch'), may hold values from -6 to 6
- rates: float32 [16, 8192], P(None, 'ch'), may hold values from 0 to 1, as said below
- residues: float32 [16, 8192], P(None, 'ch'), may hold values from -1 to 1
- skip_gain: float32 [8192], P('ch'), may hold values from -3 to 3
- norm_gain: float32 [8192], P('ch'), may hold values from 0.1 to 1.9
Outputs:
- output: bfloat16 [12288, 8192], P('seq', 'ch')
The draws below stay inside these ranges and needn't reach their ends.
Inputs may be any that keep to these rules, and one draw needn't show every extreme that they name: `rates`: each rate lies either in a slow band, between 0.1 / 12288 and 200 / 12288, or in a fast band, between 1/50 and 1/30; which modes lie in which band varies from channel to channel.
All inputs are finite; a program needn't handle non-finite values.
Results may differ from the reference program's by a relative error of at most 0.001.
Values sent between devices are 32-bit elements; how exact they have to be, the bound alone decides.
No kernel may reach another device: no remote copies, remote signals or barrier semaphores. Data moves between devices by JAX's collectives and lax.ppermute only.
A program may use at most 192 MiB of HBM per device.

```python
import math
import jax
import jax.numpy as jnp
from jax import lax

D = 8192
ORDER = 16
TOKENS = 12288


def rate_table(key, slow_share):
    first, second, third = jax.random.split(key, 3)
    slow_pick = jax.random.uniform(first, (ORDER, D)) < slow_share
    slow_rate = jnp.exp(jax.random.uniform(second, (ORDER, D), minval=math.log(0.1), maxval=math.log(200.0))) / TOKENS
    fast_rate = jnp.exp(jax.random.uniform(third, (ORDER, D), minval=math.log(1.0 / 50.0), maxval=math.log(1.0 / 30.0)))
    return jnp.where(slow_pick, slow_rate, fast_rate).astype(jnp.float32)


def draw_rates(key, part):
    return rate_table(key, 0.5)


def draw_residues(key, part):
    table = rate_table(key, 0.5)
    key = jax.random.fold_in(key, 11)
    values = jax.random.truncated_normal(key, -4.0, 4.0, (ORDER, D))
    return (values * jnp.sqrt(2.0 * table / ORDER)).astype(jnp.float32)


def draw_gate_proj(key, part):
    key = jax.random.fold_in(key, 5)
    first, second = jax.random.split(key, 2)
    columns = jnp.power(3.0, jnp.arange(D, dtype=jnp.float32) / D) * jnp.power(10.0, jax.random.uniform(second, (D,)))
    values = jax.random.truncated_normal(first, -4.0, 4.0, (TOKENS, D)) * columns[None, :]
    return values.astype(jnp.float32).astype(jnp.bfloat16)


def block_scale(key, shape, cuts, low, high):
    loudness, own = 1.0, jax.random.fold_in(key, 6)
    for position, shards_of in cuts:
        heights = jnp.exp(jax.random.uniform(jax.random.fold_in(own, position), (shards_of,), jnp.float32, low / len(cuts), high / len(cuts)))
        loudness = loudness * jnp.repeat(heights, shape[position] // shards_of).reshape([-1 if axis == position else 1 for axis in range(len(shape))])
    return loudness


def gaussian(key, dims, spread, limit, cuts=(), held_as=jnp.bfloat16):
    result = jax.random.normal(key, dims, jnp.float32) * spread
    if len(cuts) > 0:
        result = block_scale(key, dims, cuts, -0.22, 0.18) * result
    return jnp.clip(result, min=-limit, max=limit).astype(held_as)


def setup_inputs(seed: int = 0) -> dict:
    splits = jax.random.split(jax.random.key(seed), 8)
    return {
        "gate_proj": draw_gate_proj(jax.random.fold_in(splits[7], 71), 0),
        "key_proj": gaussian(splits[1], (TOKENS, D), 1.0, 6.0, ((0, 32), (1, 4))),
        "value_proj": gaussian(splits[2], (TOKENS, D), 1.0, 6.0, ((0, 32), (1, 4))),
        "rates": draw_rates(jax.random.fold_in(splits[7], 71), 0),
        "residues": draw_residues(jax.random.fold_in(splits[7], 71), 0),
        "skip_gain": gaussian(splits[5], (D,), 0.5, 3.0, ((0, 4),), jnp.float32),
        "norm_gain": jnp.clip(1.0 + 0.18 * jax.random.normal(splits[6], (D,), jnp.float32), 0.1, 1.9),
    }


def channel_block(pieces):
    signal_block, rate_block, residue_block = pieces
    positions = jnp.arange(TOKENS, dtype=jnp.float32)[:, None]
    filter_block = jnp.zeros(signal_block.shape, jnp.float32)
    for mode in range(ORDER):
        filter_block = filter_block + residue_block[mode][None, :] * jnp.exp(-rate_block[mode][None, :] * positions)
    length = 2 * TOKENS
    spectrum = jnp.fft.rfft(signal_block, n=length, axis=0) * jnp.fft.rfft(filter_block, n=length, axis=0)
    return jnp.fft.irfft(spectrum, n=length, axis=0)[:TOKENS].astype(signal_block.dtype)

def reference(gate_proj, key_proj, value_proj, rates, residues, skip_gain, norm_gain):
    block_width = 512 if D % 512 == 0 else D
    count = D // block_width
    signal = key_proj.astype(jnp.float32) * value_proj.astype(jnp.float32)
    signal_blocks = signal.reshape(TOKENS, count, block_width).transpose(1, 0, 2)
    rate_blocks = rates.reshape(ORDER, count, block_width).transpose(1, 0, 2)
    residue_blocks = residues.reshape(ORDER, count, block_width).transpose(1, 0, 2)
    conv_blocks = lax.map(channel_block, (signal_blocks, rate_blocks, residue_blocks))
    conv = conv_blocks.transpose(1, 0, 2).reshape(TOKENS, D)
    gated = gate_proj.astype(jnp.float32) * (conv + skip_gain[None, :] * signal)
    power = lax.optimization_barrier(jnp.mean(gated * gated, axis=1))
    output = gated * lax.rsqrt(power + 1e-06)[:, None] * norm_gain[None, :]
    return output.astype(jnp.bfloat16)
```

```python
import jax
import jax.numpy as jnp
from jax import lax
from jax.experimental import pallas as pl
from jax.experimental.pallas import tpu as pltpu
from jax.sharding import PartitionSpec as P

D = 8192
ORDER = 16
LANES = 128
SUB = 8
RUN = 16
OWNERS = 4
F32 = jnp.float32
BF16 = jnp.bfloat16

IN_HBM = pl.BlockSpec(memory_space=pltpu.HBM)
IN_VMEM = pl.BlockSpec(memory_space=pltpu.VMEM)
PARAMS = pltpu.CompilerParams(vmem_limit_bytes=24 << 20)


def cost(flops, bytes_accessed):
    return pl.CostEstimate(flops=flops, bytes_accessed=bytes_accessed, transcendentals=0)


def spread(table):
    return [jnp.broadcast_to(table[n : n + 1, :], (SUB, LANES)) for n in range(ORDER)]


def add_up(terms):
    terms = list(terms)
    while len(terms) > 1:
        terms = [a + b for a, b in zip(terms[::2], terms[1::2])] + terms[len(terms) & ~1 :]
    return terms[0]


def quarter_of(by):
    return lax.rem(lax.axis_index("seq") + (by + OWNERS), OWNERS)


def lanes_at(first):
    return pl.ds(pl.multiple_of(first, LANES), LANES)


def later(x, by):
    place = lax.broadcasted_iota(jnp.int32, (SUB, LANES), 0)
    return jnp.where(place >= by, pltpu.roll(x, by, 0), 0.0)


def end_of_tile(signal_ref, rates, sent_ref, ends_ref, here):
    span = signal_ref.shape[0] // SUB
    one = spread(jnp.exp(-rates))
    run = spread(jnp.exp(rates * float(-RUN)))
    total = None
    for g in range(span // RUN):
        acc = None
        for i in range(RUN):
            j = g * RUN + i
            signal = signal_ref[pl.ds(j, SUB, stride=span), :]
            sent_ref[pl.ds(j * SUB, SUB), here] = signal
            acc = [signal] * ORDER if acc is None else [a * o + signal for a, o in zip(acc, one)]
        for n in range(ORDER):
            ends_ref[pl.ds((g * ORDER + n) * SUB, SUB), here] = acc[n]
        total = acc if total is None else [t * r + a for t, r, a in zip(total, run, acc)]
    place = lax.broadcasted_iota(jnp.int32, (SUB, LANES), 0).astype(F32)
    return [
        jnp.sum(a * jnp.exp(rates[n : n + 1, :] * ((place - float(SUB - 1)) * float(span))), axis=0, keepdims=True)
        for n, a in enumerate(total)
    ]


def ends_kernel(key_ref, value_ref, rates_ref, *refs):
    outs, (key_own, value_own, key_held, value_held, signal_ref, rates_here, sems, sem) = refs[:9], refs[9:]
    width = key_own.shape[1]
    per = width // LANES
    pieces = [(quarter_of(k), j) for k in (1, 2, 3) for j in range(per)]

    def copies(i):
        quarter, j = pieces[i]
        there = lanes_at(quarter * width + j * LANES)
        return [
            pltpu.make_async_copy(a.at[:, there], b.at[i], sems.at[s, i])
            for s, (a, b) in enumerate(((key_ref, key_held), (value_ref, value_held)))
        ]

    own = pl.ds(pl.multiple_of(quarter_of(0) * width, width), width)
    own_copies = [
        pltpu.make_async_copy(a.at[:, own], b, sems.at[s, len(pieces)])
        for s, (a, b) in enumerate(((key_ref, key_own), (value_ref, value_own)))
    ]
    rates_copy = pltpu.make_async_copy(rates_ref, rates_here, sem)
    rates_copy.start()
    ahead = 4
    for i in range(ahead):
        for c in copies(i):
            c.start()
    rates_copy.wait()
    for i in range(len(pieces)):
        for c in copies(i):
            c.wait()
        if i + ahead < len(pieces):
            for c in copies(i + ahead):
                c.start()
        elif i + ahead == len(pieces):
            for c in own_copies:
                c.start()
        end_ref, sent_ref, ends_ref = outs[i // per :: 3]
        quarter, j = pieces[i]
        here = pl.ds(j * LANES, LANES)
        signal_ref[...] = key_held[i].astype(F32) * value_held[i].astype(F32)
        ends = end_of_tile(signal_ref, rates_here[:, lanes_at(quarter * width + j * LANES)], sent_ref, ends_ref, here)
        for n in range(ORDER):
            end_ref[n : n + 1, here] = ends[n]
    for c in own_copies:
        c.wait()


def far_ends(key, value, rates):
    tokens, channels = key.shape
    width = channels // OWNERS
    pieces = 3 * (width // LANES)
    end = jax.ShapeDtypeStruct((ORDER, width), F32)
    part = jax.ShapeDtypeStruct((tokens, width), F32)
    own = jax.ShapeDtypeStruct((tokens, width), BF16)
    constrained = [pltpu.with_memory_space_constraint(a, pltpu.HBM) for a in (key, value, rates)]
    return pl.pallas_call(
        ends_kernel,
        in_specs=[IN_HBM, IN_HBM, IN_HBM],
        out_specs=[IN_VMEM] * 11,
        out_shape=[end] * 3 + [part] * 6 + [own] * 2,
        scratch_shapes=[
            pltpu.VMEM((pieces, tokens, LANES), BF16),
            pltpu.VMEM((pieces, tokens, LANES), BF16),
            pltpu.VMEM((tokens, LANES), F32),
            pltpu.VMEM((ORDER, channels), F32),
            pltpu.SemaphoreType.DMA((2, pieces + 1)),
            pltpu.SemaphoreType.DMA(()),
        ],
        compiler_params=PARAMS,
        cost_estimate=cost(32 * tokens * channels, 4 * tokens * channels),
        name="far_ends",
    )(*constrained)


ENTRIES = 9


def position():
    place = lax.axis_index("seq")
    return lax.div(place, 8), lax.rem(lax.div(place, 4), 2), lax.rem(place, 4)


def own_end_kernel(key_ref, value_ref, rates_ref, end_ref, sent_ref, ends_ref, tables_ref, signal_ref):
    tokens, width = key_ref.shape
    x, z, _ = position()
    first = quarter_of(0) * width

    def tile(t, _):
        here = lanes_at(t * LANES)
        rates = rates_ref[:, lanes_at(first + t * LANES)]
        signal_ref[...] = key_ref[:, here].astype(F32) * value_ref[:, here].astype(F32)
        ends = end_of_tile(signal_ref, rates, sent_ref, ends_ref, here)
        for n in range(ORDER):
            end_ref[n : n + 1, here] = ends[n]
        rates = rates * float(-tokens)
        tables_ref[0, :, here] = jnp.zeros((ORDER, LANES), F32)
        for m in range(1, 6):
            tables_ref[m, :, here] = jnp.exp(rates * float(m - 1))
        for k in (1, 2, 3):
            spans = (4 * z + jnp.maximum(8 * (k - 1), 0)).astype(F32)
            tables_ref[5 + k, :, here] = jnp.exp(rates * spans) * (x >= k).astype(F32)
        return 0

    lax.fori_loop(0, width // LANES, tile, 0)


def own_end(key, value, rates):
    tokens, width = key.shape
    part = jax.ShapeDtypeStruct((tokens, width), F32)
    return pl.pallas_call(
        own_end_kernel,
        in_specs=[IN_VMEM] * 3,
        out_specs=[IN_VMEM] * 4,
        out_shape=[
            jax.ShapeDtypeStruct((ORDER, width), F32),
            part,
            part,
            jax.ShapeDtypeStruct((ENTRIES, ORDER, width), F32),
        ],
        scratch_shapes=[pltpu.VMEM((tokens, LANES), F32)],
        compiler_params=PARAMS,
        cost_estimate=cost(32 * tokens * width, 12 * tokens * width),
        name="own_end",
    )(key, value, rates)


def sender(y, by):
    return lax.rem(y + (OWNERS - by), OWNERS)


def row_kernel(e0, e1, e2, e3, tables_ref, row_ref):
    _, _, y = position()
    row_ref[...] = add_up([tables_ref[4 - sender(y, k)] * e[...] for k, e in enumerate((e0, e1, e2, e3))])


def plane_kernel(row_ref, other_ref, tables_ref, plane_ref):
    _, z, _ = position()
    plane_ref[...] = tables_ref[5 - 4 * z] * row_ref[...] + tables_ref[1 + 4 * z] * other_ref[...]


def states_kernel(e0, e1, e2, e3, other_ref, p1, p2, p3, tables_ref, *states):
    _, z, y = position()
    head = other_ref[...] * z.astype(F32) + add_up(
        [tables_ref[5 + k] * p[...] for k, p in ((1, p1), (2, p2), (3, p3))]
    )
    for j, state_ref in enumerate(states):
        target = lax.rem(y + j, OWNERS)
        before = [
            tables_ref[jnp.maximum(target - sender(y, k), 0)] * e[...] for k, e in enumerate((e0, e1, e2, e3))
        ]
        state_ref[...] = add_up(before) + tables_ref[1 + target] * head


def small(kernel, count, *args):
    out = jax.ShapeDtypeStruct(args[0].shape, F32)
    return pl.pallas_call(
        kernel,
        in_specs=[IN_VMEM] * len(args),
        out_specs=[IN_VMEM] * count,
        out_shape=[out] * count,
        compiler_params=PARAMS,
        cost_estimate=cost(10 * out.size, 40 * out.size),
        name=kernel.__name__,
    )(*args)


def local_kernel(by, sent_ref, ends_ref, gate_ref, rates_ref, residues_ref, skip_ref,
                 mixed_ref, gate_out, start_ref, reach_ref, enter_ref, gate_held, gate_f32, sems):
    tokens, width = mixed_ref.shape
    span = tokens // SUB
    place = lax.broadcasted_iota(jnp.int32, (SUB, LANES), 0).astype(F32)

    def copy(t):
        there = lanes_at(quarter_of(by) * width + t * LANES)
        return pltpu.make_async_copy(gate_ref.at[:, there], gate_held.at[t], sems.at[t])

    for t in range(width // LANES):
        copy(t).start()

    def tile(t, _):
        lanes = lanes_at(quarter_of(by) * width + t * LANES)
        here = lanes_at(t * LANES)
        rates = rates_ref[:, lanes]
        residues = residues_ref[:, lanes]
        decay = jnp.exp(-rates)

        taps, term = [], residues
        for k in range(RUN):
            tap = term[:SUB] + term[SUB:]
            for shift in (4, 2, 1):
                tap = tap + pltpu.roll(tap, shift, 0)
            taps.append(tap)
            term = term * decay
        taps[0] = taps[0] + skip_ref[:, lanes]

        run = spread(jnp.exp(rates * float(-RUN)))

        def end(g, n):
            return ends_ref[pl.ds((g * ORDER + n) * SUB, SUB), here]

        state = [(end(0, n) * run[n] + end(1, n)) * run[n] + end(2, n) for n in range(ORDER)]
        for step in (1, 2, 4):
            across = spread(jnp.exp(rates * float(-span * step)))
            state = [s + later(s, step) * a for s, a in zip(state, across)]
        first = spread(residues * decay)
        for n in range(ORDER):
            rows = pl.ds(n * SUB, SUB)
            start_ref[rows, here] = first[n] * later(state[n], 1)
            reach_ref[rows, here] = first[n] * jnp.exp(rates[n : n + 1, :] * (place * float(-span)))
            for g in (0, 1):
                enter_ref[pl.ds((g * ORDER + n) * SUB, SUB), here] = first[n] * end(g, n)

        copy(t).wait()
        gate_f32[...] = gate_held[t].astype(F32)

        def group(g, _):
            signal = []
            for i in range(RUN):
                rows = pl.ds(pl.multiple_of((g * RUN + i) * SUB, SUB), SUB)
                signal.append(sent_ref[rows, here])
                gate = gate_f32[pl.ds(g * RUN + i, SUB, stride=span), :]
                conv = add_up([taps[i - m] * signal[m] for m in range(i + 1)])
                mixed_ref[rows, here] = gate * conv
                gate_out[rows, here] = gate
            return 0

        lax.fori_loop(0, span // RUN, group, 0)
        return 0

    lax.fori_loop(0, width // LANES, tile, 0)


def local_part(by, sent, ends, gate, rates, residues, skip):
    tokens, width = sent.shape
    token_part = jax.ShapeDtypeStruct((tokens, width), F32)
    mode_part = jax.ShapeDtypeStruct((ORDER * SUB, width), F32)
    enter_part = jax.ShapeDtypeStruct((2 * ORDER * SUB, width), F32)
    gate = pltpu.with_memory_space_constraint(gate, pltpu.HBM)
    return pl.pallas_call(
        lambda *refs: local_kernel(by, *refs),
        in_specs=[IN_VMEM, IN_VMEM, IN_HBM, IN_VMEM, IN_VMEM, IN_VMEM],
        out_specs=[IN_VMEM] * 5,
        out_shape=[token_part, token_part, mode_part, mode_part, enter_part],
        scratch_shapes=[
            pltpu.VMEM((width // LANES, tokens, LANES), BF16),
            pltpu.VMEM((tokens, LANES), F32),
            pltpu.SemaphoreType.DMA((width // LANES,)),
        ],
        compiler_params=PARAMS,
        cost_estimate=cost(30 * tokens * width, 14 * tokens * width),
        name="local_part",
    )(sent, ends, gate, rates, residues, skip)


def mix_kernel(by, last, mixed_ref, gate_ref, start_ref, reach_ref, enter_ref, state_ref, rates_ref, *rest):
    tokens, width = mixed_ref.shape
    span = tokens // SUB
    gated_ref, sums_ref = rest[-2], rest[-1]
    if by == 0:
        sums_ref[...] = jnp.zeros_like(sums_ref)
    else:
        sums_ref[...] = rest[0][...]
    if last:
        power_ref = rest[1]

    def tile(t, _):
        here = lanes_at(t * LANES)
        step = spread(jnp.exp(-rates_ref[:, lanes_at(quarter_of(-by) * width + t * LANES)]))
        state = state_ref[:, here]
        terms = []
        for n in range(ORDER):
            rows = pl.ds(n * SUB, SUB)
            terms.append(start_ref[rows, here] + reach_ref[rows, here] * state[n : n + 1, :])
        for j in range(span):
            if j > 0:
                terms = [a * b for a, b in zip(terms, step)]
            if j > 0 and j % RUN == 0:
                g = j // RUN - 1
                terms = [a + enter_ref[pl.ds((g * ORDER + n) * SUB, SUB), here] for n, a in enumerate(terms)]
            rows = pl.ds(j * SUB, SUB)
            gated = mixed_ref[rows, here] + gate_ref[rows, here] * add_up(terms)
            gated_ref[t, pl.ds(j, SUB, stride=span), :] = gated
            sums_ref[rows, :] += gated * gated
        return 0

    lax.fori_loop(0, width // LANES, tile, 0)
    if last:
        power_ref[...] = lax.dot_general(
            jnp.ones((SUB, LANES), F32),
            sums_ref[...],
            (((1,), (1,)), ((), ())),
            precision=lax.Precision.HIGHEST,
            preferred_element_type=F32,
        )[0:1, :]


def mix(by, last, part, state, rates, sums):
    tokens, width = part[0].shape
    out_sums = jax.ShapeDtypeStruct((tokens, LANES), F32)
    gated = jax.ShapeDtypeStruct((width // LANES, tokens, LANES), F32)
    args = [*part, state, rates] + ([] if sums is None else [sums])
    if last:
        outs, scratch = [jax.ShapeDtypeStruct((1, tokens), F32), gated], [pltpu.VMEM((tokens, LANES), F32)]
    else:
        outs, scratch = [gated, out_sums], []
    return pl.pallas_call(
        lambda *refs: mix_kernel(by, last, *refs),
        in_specs=[IN_VMEM] * len(args),
        out_specs=[IN_VMEM] * 2,
        out_shape=outs,
        scratch_shapes=scratch,
        compiler_params=PARAMS,
        cost_estimate=cost(40 * tokens * width, 12 * tokens * width),
        name="mix",
    )(*args)


def norm_kernel(g0, g1, g2, g3, gain_ref, p0_ref, p1_ref, p2_ref, p3_ref, out_ref, runs_ref, scale_ref, held, sems):
    tiles, tokens, _ = g0.shape
    width = tiles * LANES
    span = tokens // SUB
    total = (p0_ref[...] + p1_ref[...]) + (p2_ref[...] + p3_ref[...])
    first = (lax.broadcasted_iota(jnp.int32, (SUB, LANES), 0) == 0).astype(F32)
    power = lax.dot_general(
        jnp.broadcast_to(total, (SUB, tokens)),
        first,
        (((0,), (0,)), ((), ())),
        precision=lax.Precision.HIGHEST,
        preferred_element_type=F32,
    )
    runs_ref[...] = lax.rsqrt(power * (1.0 / D) + 1e-6)
    for i in range(span):
        scale_ref[pl.ds(i, SUB, stride=span), :] = runs_ref[pl.ds(i * SUB, SUB), :]

    copies = []
    for by, gated_ref in enumerate((g0, g1, g2, g3)):
        first = quarter_of(-by) * width

        def tile(t, _):
            here = lanes_at(t * LANES)
            gain = gain_ref[:, lanes_at(first + t * LANES)]
            held[by, :, here] = (gated_ref[t] * scale_ref[...] * gain).astype(BF16)
            return 0

        lax.fori_loop(0, width // LANES, tile, 0)
        copy = pltpu.make_async_copy(
            held.at[by], out_ref.at[:, pl.ds(pl.multiple_of(first, width), width)], sems.at[by]
        )
        copy.start()
        copies.append(copy)
    for copy in copies:
        copy.wait()


def norm(gated, gain, powers):
    tiles, tokens, _ = gated[0].shape
    width = tiles * LANES
    channels = width * OWNERS
    return pl.pallas_call(
        norm_kernel,
        in_specs=[IN_VMEM] * 9,
        out_specs=IN_HBM,
        out_shape=jax.ShapeDtypeStruct((tokens, channels), BF16),
        scratch_shapes=[
            pltpu.VMEM((tokens, LANES), F32),
            pltpu.VMEM((tokens, LANES), F32),
            pltpu.VMEM((OWNERS, tokens, width), BF16),
            pltpu.SemaphoreType.DMA((OWNERS,)),
        ],
        compiler_params=PARAMS,
        cost_estimate=cost(3 * tokens * channels, 6 * tokens * channels),
        name="norm",
    )(*gated, gain, *powers)


def over_y(x, by):
    return lax.ppermute(x, "seq", [(i, i // 4 * 4 + (i + by) % 4) for i in range(32)])


def over_z(x):
    return lax.ppermute(x, "seq", [(i, i ^ 4) for i in range(32)])


def over_x(x, by):
    return lax.ppermute(x, "seq", [(i, (i + 8 * by) % 32) for i in range(32)])


def over_ch(x, by):
    return lax.ppermute(x, "ch", [(i, (i + by) % 4) for i in range(4)])


def body(gate, key, value, rates, residues, skip_gain, norm_gain):
    skip = skip_gain[None, :]
    tie = lax.optimization_barrier
    parts = [None] * OWNERS

    def local(by, rates):
        parts[by] = local_part(-by, sent[-by], inner[-by], gate, rates, residues, skip)

    outs = far_ends(key, value, rates)
    ends, sent, inner = [None, *outs[0:3]], [None, *outs[3:6]], [None, *outs[6:9]]
    got = [over_y(ends[k], k) for k in (1, 2, 3)]
    own, sent[0], inner[0], tables = own_end(*outs[9:11], rates)
    local(1, rates)
    own, parts[1] = tie((own, parts[1]))
    ends = [own] + got
    (row,) = small(row_kernel, 1, *ends, tables)

    row, rates1 = tie((row, rates))
    other = over_z(row)
    local(2, rates1)
    local(3, rates1)
    other, parts[2], parts[3] = tie((other, parts[2], parts[3]))
    (plane,) = small(plane_kernel, 1, row, other, tables)

    plane, rates2 = tie((plane, rates))
    got = [over_x(plane, k) for k in (1, 2, 3)]
    local(0, rates2)
    got[0], parts[0] = tie((got[0], parts[0]))
    states = list(small(states_kernel, OWNERS, *ends, other, *got, tables))

    states = [states[0]] + [over_y(s, k) for k, s in zip((1, 2, 3), states[1:])]
    gated, sums = [], None
    for by in range(OWNERS):
        first, second = mix(by, by == OWNERS - 1, parts[by], states[by], rates, sums)
        if by < OWNERS - 1:
            gated.append(first)
            sums = second
        else:
            gated.append(second)
            power = first
    powers = [power] + [over_ch(power, k) for k in (1, 2, 3)]
    return norm(gated, norm_gain[None, :], powers)


def solution(mesh):
    placed = (
        P("seq", "ch"),
        P("seq", "ch"),
        P("seq", "ch"),
        P(None, "ch"),
        P(None, "ch"),
        P("ch"),
        P("ch"),
    )
    return jax.shard_map(
        body, mesh=mesh, in_specs=placed, out_specs=P("seq", "ch"), check_vma=False
    )
```

```python
import jax
import jax.numpy as jnp
from jax import lax
from jax.experimental import pallas as pl
from jax.experimental.pallas import tpu as pltpu
from jax.sharding import PartitionSpec as P

D = 8192
ORDER = 16
LANES = 128
SUB = 8
RUN = 16
PITCH = 52
OUT_PITCH = 50
OWNERS = 4
F32 = jnp.float32
BF16 = jnp.bfloat16

IN_HBM = pl.BlockSpec(memory_space=pltpu.HBM)
IN_VMEM = pl.BlockSpec(memory_space=pltpu.VMEM)
PARAMS = pltpu.CompilerParams(vmem_limit_bytes=24 << 20)


def cost(us):
    return pl.CostEstimate(flops=int(us * 1.15e9), bytes_accessed=int(us * 3.69e6), transcendentals=0)


def spread(table):
    return [jnp.broadcast_to(table[n : n + 1, :], (SUB, LANES)) for n in range(ORDER)]


def add_up(terms):
    terms = list(terms)
    while len(terms) > 1:
        terms = [a + b for a, b in zip(terms[::2], terms[1::2])] + terms[len(terms) & ~1 :]
    return terms[0]


def quarter_of(by):
    return lax.rem(lax.axis_index("seq") + (by + OWNERS), OWNERS)


def lanes_at(first):
    return pl.ds(pl.multiple_of(first, LANES), LANES)


def later(x, by):
    place = lax.broadcasted_iota(jnp.int32, (SUB, LANES), 0)
    return jnp.where(place >= by, pltpu.roll(x, by, 0), 0.0)


def end_of_tile(span, signal_ref, rates, sent_ref, ends_ref, here):
    one = spread(jnp.exp(-rates))
    run = spread(jnp.exp(rates * float(-RUN)))
    total = None
    for g in range(span // RUN):
        acc = None
        for i in range(RUN):
            j = g * RUN + i
            signal = signal_ref[pl.ds(j, SUB, stride=PITCH), :]
            sent_ref[pl.ds(j * SUB, SUB), here] = signal
            acc = [signal] * ORDER if acc is None else [a * o + signal for a, o in zip(acc, one)]
        for n in range(ORDER):
            ends_ref[pl.ds((g * ORDER + n) * SUB, SUB), here] = acc[n]
        total = acc if total is None else [t * r + a for t, r, a in zip(total, run, acc)]
    for by in (1, 2, 4):
        across = spread(jnp.exp(rates * float(-span * by)))
        total = [t + pltpu.roll(t, by, 0) * a for t, a in zip(total, across)]
    return [t[SUB - 1 :, :] for t in total]


def end_of_piece(key_ref, value_ref, rates_ref, first, signal_ref, sent_ref, ends_ref, end_ref, at):
    span = key_ref.shape[0] // SUB

    def tile(t, _):
        there, here = lanes_at(t * LANES), lanes_at(at + t * LANES)
        for s in range(SUB):
            rows = pl.ds(s * span, span)
            signal_ref[pl.ds(s * PITCH, span), :] = key_ref[rows, there].astype(F32) * value_ref[rows, there].astype(F32)
        ends = end_of_tile(span, signal_ref, rates_ref[:, lanes_at(first + t * LANES)], sent_ref, ends_ref, here)
        for n in range(ORDER):
            end_ref[n : n + 1, here] = ends[n]
        return 0

    lax.fori_loop(0, key_ref.shape[1] // LANES, tile, 0)


def quarter_copies(by, sources, targets, sems, cuts):
    width = targets[0].shape[1]
    step = width // cuts
    return [
        [
            pltpu.make_async_copy(
                a.at[:, pl.ds(pl.multiple_of(quarter_of(by) * width + j * step, step), step)],
                b.at[:, pl.ds(j * step, step)],
                sems.at[s, j],
            )
            for s, (a, b) in enumerate(zip(sources, targets))
        ]
        for j in range(cuts)
    ]


def far_ends_kernel(key_ref, value_ref, rates_ref, *refs):
    results, (key_held, value_held, signal_ref, rates_here, sems, sem) = refs[:9], refs[9:]
    width = key_held.shape[2]
    cuts = 2
    step = width // cuts
    sources = (key_ref, value_ref)
    pieces = []
    for by in (1, 2, 3):
        pieces += quarter_copies(by, sources, (key_held.at[by - 1], value_held.at[by - 1]), sems.at[by - 1], cuts)
    rates_copy = pltpu.make_async_copy(rates_ref, rates_here, sem)
    rates_copy.start()
    ahead = 3
    for i in range(ahead):
        for c in pieces[i]:
            c.start()
    rates_copy.wait()
    for i in range(3 * cuts):
        for c in pieces[i]:
            c.wait()
        if i + ahead < len(pieces):
            for c in pieces[i + ahead]:
                c.start()
        by, at = i // cuts, i % cuts * step
        end_ref, sent_ref, ends_ref = results[3 * by : 3 * by + 3]
        part = pl.ds(at, step)
        end_of_piece(key_held.at[by, :, part], value_held.at[by, :, part], rates_here,
                     quarter_of(by + 1) * width + at, signal_ref, sent_ref, ends_ref, end_ref, at)


def end_shapes(tokens, width):
    part = jax.ShapeDtypeStruct((tokens, width), F32)
    return [jax.ShapeDtypeStruct((ORDER, width), F32), part, part]


def in_hbm(*arrays):
    return [pltpu.with_memory_space_constraint(a, pltpu.HBM) for a in arrays]


def far_ends(key, value, rates):
    tokens, channels = key.shape
    width = channels // OWNERS
    return pl.pallas_call(
        far_ends_kernel,
        in_specs=[IN_HBM] * 3,
        out_specs=[IN_VMEM] * 9,
        out_shape=end_shapes(tokens, width) * 3,
        scratch_shapes=[
            pltpu.VMEM((3, tokens, width), BF16),
            pltpu.VMEM((3, tokens, width), BF16),
            pltpu.VMEM((SUB * PITCH, LANES), F32),
            pltpu.VMEM((ORDER, channels), F32),
            pltpu.SemaphoreType.DMA((3, 2, 2)),
            pltpu.SemaphoreType.DMA(()),
        ],
        compiler_params=PARAMS,
        cost_estimate=cost(4.6),
        name="far_ends",
    )(*in_hbm(key, value, rates))


ENTRIES = 9


def position():
    place = lax.axis_index("seq")
    return lax.div(place, 8), lax.rem(lax.div(place, 4), 2), lax.rem(place, 4)


def own_end_kernel(key_ref, value_ref, rates_ref, end_ref, sent_ref, ends_ref, tables_ref,
                   key_held, value_held, signal_ref, sems):
    tokens, width = key_held.shape
    x, z, _ = position()
    first = quarter_of(0) * width
    (copies,) = quarter_copies(0, (key_ref, value_ref), (key_held, value_held), sems, 1)
    for c in copies:
        c.start()

    def table(t, _):
        here = lanes_at(t * LANES)
        rates = rates_ref[:, lanes_at(first + t * LANES)] * float(-tokens)
        tables_ref[0, :, here] = jnp.zeros((ORDER, LANES), F32)
        for m in range(1, 6):
            tables_ref[m, :, here] = jnp.exp(rates * float(m - 1))
        for k in (1, 2, 3):
            spans = (4 * z + 8 * (k - 1)).astype(F32)
            tables_ref[5 + k, :, here] = jnp.exp(rates * spans) * (x >= k).astype(F32)
        return 0

    lax.fori_loop(0, width // LANES, table, 0)
    for c in copies:
        c.wait()
    end_of_piece(key_held, value_held, rates_ref, first, signal_ref, sent_ref, ends_ref, end_ref, 0)


def own_end(key, value, rates):
    tokens, channels = key.shape
    width = channels // OWNERS
    return pl.pallas_call(
        own_end_kernel,
        in_specs=[IN_HBM, IN_HBM, IN_VMEM],
        out_specs=[IN_VMEM] * 4,
        out_shape=end_shapes(tokens, width) + [jax.ShapeDtypeStruct((ENTRIES, ORDER, width), F32)],
        scratch_shapes=[
            pltpu.VMEM((tokens, width), BF16),
            pltpu.VMEM((tokens, width), BF16),
            pltpu.VMEM((SUB * PITCH, LANES), F32),
            pltpu.SemaphoreType.DMA((2, 1)),
        ],
        compiler_params=PARAMS,
        cost_estimate=cost(2.3),
        name="own_end",
    )(*in_hbm(key, value), rates)


def sender(y, by):
    return lax.rem(y + (OWNERS - by), OWNERS)


def row_kernel(e0, e1, e2, e3, tables_ref, row_ref):
    _, _, y = position()
    row_ref[...] = add_up([tables_ref[4 - sender(y, k)] * e[...] for k, e in enumerate((e0, e1, e2, e3))])


def plane_kernel(row_ref, other_ref, tables_ref, plane_ref):
    _, z, _ = position()
    plane_ref[...] = tables_ref[5 - 4 * z] * row_ref[...] + tables_ref[1 + 4 * z] * other_ref[...]


def states_kernel(e0, e1, e2, e3, other_ref, p1, p2, p3, tables_ref, *states):
    _, z, y = position()
    head = other_ref[...] * z.astype(F32) + add_up(
        [tables_ref[5 + k] * p[...] for k, p in ((1, p1), (2, p2), (3, p3))]
    )
    for j, state_ref in enumerate(states):
        target = lax.rem(y + j, OWNERS)
        before = [
            tables_ref[jnp.maximum(target - sender(y, k), 0)] * e[...] for k, e in enumerate((e0, e1, e2, e3))
        ]
        state_ref[...] = add_up(before) + tables_ref[1 + target] * head


def small(kernel, count, *args):
    out = jax.ShapeDtypeStruct(args[0].shape, F32)
    return pl.pallas_call(
        kernel,
        in_specs=[IN_VMEM] * len(args),
        out_specs=[IN_VMEM] * count,
        out_shape=[out] * count,
        compiler_params=PARAMS,
        cost_estimate=cost(0.05),
        name=kernel.__name__,
    )(*args)


def local_kernel(by, sent_ref, ends_ref, gate_ref, rates_ref, residues_ref, skip_ref,
                 mixed_ref, gate_out, start_ref, reach_ref, enter_ref, gate_held, gate_f32, sems):
    tokens, width = mixed_ref.shape
    span = tokens // SUB
    place = lax.broadcasted_iota(jnp.int32, (SUB, LANES), 0).astype(F32)

    def copy(t):
        there = lanes_at(quarter_of(-by) * width + t * LANES)
        return pltpu.make_async_copy(gate_ref.at[:, there], gate_held.at[t], sems.at[t])

    for t in range(width // LANES):
        copy(t).start()

    def tile(t, _):
        lanes = lanes_at(quarter_of(-by) * width + t * LANES)
        here = lanes_at(t * LANES)
        rates = rates_ref[:, lanes]
        residues = residues_ref[:, lanes]
        decay = jnp.exp(-rates)

        taps, term = [], residues
        for k in range(RUN):
            tap = term[:SUB] + term[SUB:]
            for shift in (4, 2, 1):
                tap = tap + pltpu.roll(tap, shift, 0)
            taps.append(tap)
            term = term * decay
        taps[0] = taps[0] + skip_ref[:, lanes]

        run = spread(jnp.exp(rates * float(-RUN)))

        def end(g, n):
            return ends_ref[pl.ds((g * ORDER + n) * SUB, SUB), here]

        state = [(end(0, n) * run[n] + end(1, n)) * run[n] + end(2, n) for n in range(ORDER)]
        for step in (1, 2, 4):
            across = spread(jnp.exp(rates * float(-span * step)))
            state = [s + later(s, step) * a for s, a in zip(state, across)]
        first = spread(residues * decay)
        for n in range(ORDER):
            rows = pl.ds(n * SUB, SUB)
            start_ref[rows, here] = first[n] * later(state[n], 1)
            reach_ref[rows, here] = first[n] * jnp.exp(rates[n : n + 1, :] * (place * float(-span)))
            for g in (0, 1):
                enter_ref[pl.ds((g * ORDER + n) * SUB, SUB), here] = first[n] * end(g, n)

        def group(g, _):
            signal = []
            for i in range(RUN):
                rows = pl.ds(pl.multiple_of((g * RUN + i) * SUB, SUB), SUB)
                signal.append(sent_ref[rows, here])
                mixed_ref[rows, here] = add_up([taps[i - m] * signal[m] for m in range(i + 1)])
            return 0

        lax.fori_loop(0, span // RUN, group, 0)
        return 0

    def gating(t, _):
        here = lanes_at(t * LANES)
        copy(t).wait()
        for s in range(SUB):
            gate_f32[pl.ds(s * PITCH, span), :] = gate_held[t, pl.ds(s * span, span), :].astype(F32)
        for j in range(span):
            rows = pl.ds(j * SUB, SUB)
            gate = gate_f32[pl.ds(j, SUB, stride=PITCH), :]
            mixed_ref[rows, here] = gate * mixed_ref[rows, here]
            gate_out[rows, here] = gate
        return 0

    lax.fori_loop(0, width // LANES, tile, 0)
    lax.fori_loop(0, width // LANES, gating, 0)


def local_part(by, sent, ends, gate, rates, residues, skip):
    tokens, width = sent.shape
    token_part = jax.ShapeDtypeStruct((tokens, width), F32)
    mode_part = jax.ShapeDtypeStruct((ORDER * SUB, width), F32)
    enter_part = jax.ShapeDtypeStruct((2 * ORDER * SUB, width), F32)
    gate = pltpu.with_memory_space_constraint(gate, pltpu.HBM)
    return pl.pallas_call(
        lambda *refs: local_kernel(by, *refs),
        in_specs=[IN_VMEM, IN_VMEM, IN_HBM, IN_VMEM, IN_VMEM, IN_VMEM],
        out_specs=[IN_VMEM] * 5,
        out_shape=[token_part, token_part, mode_part, mode_part, enter_part],
        scratch_shapes=[
            pltpu.VMEM((width // LANES, tokens, LANES), BF16),
            pltpu.VMEM((SUB * PITCH, LANES), F32),
            pltpu.SemaphoreType.DMA((width // LANES,)),
        ],
        compiler_params=PARAMS,
        cost_estimate=cost(1.4),
        name="local_part",
    )(sent, ends, gate, rates, residues, skip)


def mix_kernel(by, last, mixed_ref, gate_ref, start_ref, reach_ref, enter_ref, state_ref, rates_ref, *rest):
    tokens, width = mixed_ref.shape
    span = tokens // SUB
    gated_ref, sums_ref = rest[-2], rest[-1]
    if by == 0:
        sums_ref[...] = jnp.zeros_like(sums_ref)
    else:
        sums_ref[...] = rest[0][...]
    if last:
        power_ref = rest[1]

    def tile(t, _):
        here = lanes_at(t * LANES)
        step = spread(jnp.exp(-rates_ref[:, lanes_at(quarter_of(-by) * width + t * LANES)]))
        state = state_ref[:, here]
        terms = []
        for n in range(ORDER):
            rows = pl.ds(n * SUB, SUB)
            terms.append(start_ref[rows, here] + reach_ref[rows, here] * state[n : n + 1, :])
        for j in range(span):
            if j > 0:
                terms = [a * b for a, b in zip(terms, step)]
            if j > 0 and j % RUN == 0:
                g = j // RUN - 1
                terms = [a + enter_ref[pl.ds((g * ORDER + n) * SUB, SUB), here] for n, a in enumerate(terms)]
            rows = pl.ds(j * SUB, SUB)
            gated = mixed_ref[rows, here] + gate_ref[rows, here] * add_up(terms)
            gated_ref[t, pl.ds(j, SUB, stride=OUT_PITCH), :] = gated
            sums_ref[rows, :] += gated * gated
        return 0

    lax.fori_loop(0, width // LANES, tile, 0)
    if last:
        power_ref[...] = lax.dot_general(
            jnp.ones((SUB, LANES), F32),
            sums_ref[...],
            (((1,), (1,)), ((), ())),
            precision=lax.Precision.HIGHEST,
            preferred_element_type=F32,
        )[0:1, :]


def mix(by, last, part, state, rates, sums):
    tokens, width = part[0].shape
    out_sums = jax.ShapeDtypeStruct((tokens, LANES), F32)
    gated = jax.ShapeDtypeStruct((width // LANES, SUB * OUT_PITCH, LANES), F32)
    args = [*part, state, rates] + ([] if sums is None else [sums])
    if last:
        outs, scratch = [jax.ShapeDtypeStruct((1, tokens), F32), gated], [pltpu.VMEM((tokens, LANES), F32)]
    else:
        outs, scratch = [gated, out_sums], []
    return pl.pallas_call(
        lambda *refs: mix_kernel(by, last, *refs),
        in_specs=[IN_VMEM] * len(args),
        out_specs=[IN_VMEM] * 2,
        out_shape=outs,
        scratch_shapes=scratch,
        compiler_params=PARAMS,
        cost_estimate=cost(1.1),
        name="mix",
    )(*args)


def norm_kernel(g0, g1, g2, g3, gain_ref, p0_ref, p1_ref, p2_ref, p3_ref, out_ref, runs_ref, scale_ref, held, sems):
    tiles, tokens = g0.shape[0], scale_ref.shape[0]
    width = tiles * LANES
    span = tokens // SUB
    total = (p0_ref[...] + p1_ref[...]) + (p2_ref[...] + p3_ref[...])
    first = (lax.broadcasted_iota(jnp.int32, (SUB, LANES), 0) == 0).astype(F32)
    power = lax.dot_general(
        jnp.broadcast_to(total, (SUB, tokens)),
        first,
        (((0,), (0,)), ((), ())),
        precision=lax.Precision.HIGHEST,
        preferred_element_type=F32,
    )
    runs_ref[...] = lax.rsqrt(power * (1.0 / D) + 1e-6)
    for i in range(span):
        scale_ref[pl.ds(i, SUB, stride=span), :] = runs_ref[pl.ds(i * SUB, SUB), :]

    copies = []
    for by, gated_ref in enumerate((g0, g1, g2, g3)):
        first = quarter_of(-by) * width

        def tile(t, _):
            here = lanes_at(t * LANES)
            gain = gain_ref[:, lanes_at(first + t * LANES)]
            for s in range(SUB):
                rows = pl.ds(s * span, span)
                gated = gated_ref[t, pl.ds(s * OUT_PITCH, span), :]
                held[by, rows, here] = (gated * scale_ref[rows, :] * gain).astype(BF16)
            return 0

        lax.fori_loop(0, width // LANES, tile, 0)
        copy = pltpu.make_async_copy(
            held.at[by], out_ref.at[:, pl.ds(pl.multiple_of(first, width), width)], sems.at[by]
        )
        copy.start()
        copies.append(copy)
    for copy in copies:
        copy.wait()


def norm(gated, gain, powers):
    tiles, tokens = gated[0].shape[0], powers[0].shape[1]
    width = tiles * LANES
    channels = width * OWNERS
    return pl.pallas_call(
        norm_kernel,
        in_specs=[IN_VMEM] * 9,
        out_specs=IN_HBM,
        out_shape=jax.ShapeDtypeStruct((tokens, channels), BF16),
        scratch_shapes=[
            pltpu.VMEM((tokens, LANES), F32),
            pltpu.VMEM((tokens, LANES), F32),
            pltpu.VMEM((OWNERS, tokens, width), BF16),
            pltpu.SemaphoreType.DMA((OWNERS,)),
        ],
        compiler_params=PARAMS,
        cost_estimate=cost(1.7),
        name="norm",
    )(*gated, gain, *powers)


def over_y(x, by):
    return lax.ppermute(x, "seq", [(i, i // 4 * 4 + (i + by) % 4) for i in range(32)])


def over_z(x):
    return lax.ppermute(x, "seq", [(i, i ^ 4) for i in range(32)])


def over_x(x, by):
    return lax.ppermute(x, "seq", [(i, (i + 8 * by) % 32) for i in range(32)])


def over_ch(x, by):
    return lax.ppermute(x, "ch", [(i, (i + by) % 4) for i in range(4)])


def body(gate, key, value, rates, residues, skip_gain, norm_gain):
    skip = skip_gain[None, :]
    tie = lax.optimization_barrier
    parts = [None] * OWNERS

    def local(by, rates):
        parts[by] = local_part(by, sent[-by], inner[-by], gate, rates, residues, skip)

    ends, sent, inner = ([None] * OWNERS for _ in range(3))
    outs = far_ends(key, value, rates)
    ends[1:], sent[1:], inner[1:] = outs[0::3], outs[1::3], outs[2::3]
    ends[1], rates0 = tie((ends[1], rates))
    for k in (2, 1, 3):
        ends[k] = over_y(ends[k], k)
    ends[0], sent[0], inner[0], tables = own_end(key, value, rates0)
    (row,) = small(row_kernel, 1, *ends, tables)

    row, rates1 = tie((row, rates))
    other = over_z(row)
    for by in (1, 2, 3):
        local(by, rates1)
    other, *parts[1:] = tie((other, *parts[1:]))
    (plane,) = small(plane_kernel, 1, row, other, tables)

    plane, rates2 = tie((plane, rates))
    got = {k: over_x(plane, k) for k in (2, 1, 3)}
    got = [got[k] for k in (1, 2, 3)]
    local(0, rates2)
    got[0], parts[0] = tie((got[0], parts[0]))
    states = list(small(states_kernel, OWNERS, *ends, other, *got, tables))

    for k in (2, 1, 3):
        states[k] = over_y(states[k], k)
    gated, sums = [], None
    for by in range(OWNERS):
        first, second = mix(by, by == OWNERS - 1, parts[by], states[by], rates, sums)
        if by < OWNERS - 1:
            gated.append(first)
            sums = second
        else:
            gated.append(second)
            power = first
    powers = [power] + [over_ch(power, k) for k in (1, 2, 3)]
    return norm(gated, norm_gain[None, :], powers)


def solution(mesh):
    placed = (
        P("seq", "ch"),
        P("seq", "ch"),
        P("seq", "ch"),
        P(None, "ch"),
        P(None, "ch"),
        P("ch"),
        P("ch"),
    )
    return jax.shard_map(
        body, mesh=mesh, in_specs=placed, out_specs=P("seq", "ch"), check_vma=False
    )
```

```python
import jax
import jax.numpy as jnp
from jax import lax
from jax.experimental import pallas as pl
from jax.experimental.pallas import tpu as pltpu
from jax.sharding import PartitionSpec as P

D = 8192
ORDER = 16
LANES = 128
SUB = 8
RUN = 16
PITCH = 52
OUT_PITCH = 50
OWNERS = 2
F32 = jnp.float32
BF16 = jnp.bfloat16

IN_HBM = pl.BlockSpec(memory_space=pltpu.HBM)
IN_VMEM = pl.BlockSpec(memory_space=pltpu.VMEM)
PARAMS = pltpu.CompilerParams(vmem_limit_bytes=24 << 20)


def cost(us):
    return pl.CostEstimate(flops=int(us * 1.15e9), bytes_accessed=int(us * 3.69e6), transcendentals=0)


def spread(table):
    return [jnp.broadcast_to(table[n : n + 1, :], (SUB, LANES)) for n in range(ORDER)]


def add_up(terms):
    terms = list(terms)
    while len(terms) > 1:
        terms = [a + b for a, b in zip(terms[::2], terms[1::2])] + terms[len(terms) & ~1 :]
    return terms[0]


def position():
    place = lax.axis_index("seq")
    return lax.div(place, 8), lax.rem(lax.div(place, 4), 2), lax.rem(lax.div(place, 2), 2), lax.rem(place, 2)


def half_of(by):
    _, _, pair, odd = position()
    return lax.rem(pair + odd + by, 2)


def lanes_at(first):
    return pl.ds(pl.multiple_of(first, LANES), LANES)


def later(x, by):
    place = lax.broadcasted_iota(jnp.int32, (SUB, LANES), 0)
    return jnp.where(place >= by, pltpu.roll(x, by, 0), 0.0)


def end_of_tile(span, signal_ref, rates, sent_ref, ends_ref, here):
    one = spread(jnp.exp(-rates))
    run = spread(jnp.exp(rates * float(-RUN)))
    total = None
    for g in range(span // RUN):
        acc = None
        for i in range(RUN):
            j = g * RUN + i
            signal = signal_ref[pl.ds(j, SUB, stride=PITCH), :]
            sent_ref[pl.ds(j * SUB, SUB), here] = signal
            acc = [signal] * ORDER if acc is None else [a * o + signal for a, o in zip(acc, one)]
        for n in range(ORDER):
            ends_ref[pl.ds((g * ORDER + n) * SUB, SUB), here] = acc[n]
        total = acc if total is None else [t * r + a for t, r, a in zip(total, run, acc)]
    for by in (1, 2, 4):
        across = spread(jnp.exp(rates * float(-span * by)))
        total = [t + pltpu.roll(t, by, 0) * a for t, a in zip(total, across)]
    return [t[SUB - 1 :, :] for t in total]


def end_of_piece(key_ref, value_ref, rates_ref, first, signal_ref, sent_ref, ends_ref, end_ref, at):
    span = key_ref.shape[0] // SUB

    def tile(t, _):
        there, here = lanes_at(t * LANES), lanes_at(at + t * LANES)
        for s in range(SUB):
            rows = pl.ds(s * span, span)
            signal_ref[pl.ds(s * PITCH, span), :] = key_ref[rows, there].astype(F32) * value_ref[rows, there].astype(F32)
        ends = end_of_tile(span, signal_ref, rates_ref[:, lanes_at(first + t * LANES)], sent_ref, ends_ref, here)
        for n in range(ORDER):
            end_ref[n : n + 1, here] = ends[n]
        return 0

    lax.fori_loop(0, key_ref.shape[1] // LANES, tile, 0)


def half_copies(by, sources, targets, sems, cuts, which):
    width = sources[0].shape[1] // OWNERS
    step = width // cuts
    return [
        [
            pltpu.make_async_copy(
                a.at[:, pl.ds(pl.multiple_of(half_of(by) * width + j * step, step), step)],
                b.at[:, pl.ds(j * step, step)],
                sems.at[s, j],
            )
            for s, (a, b) in enumerate(zip(sources, targets))
        ]
        for j in which
    ]


def far_end_kernel(key_ref, value_ref, rates_ref, end_ref, sent_ref, ends_ref, key_own, value_own,
                   key_held, value_held, signal_ref, rates_here, sems, sem):
    width = key_held.shape[1]
    cuts = 4
    step = width // cuts
    sources = (key_ref, value_ref)
    pieces = half_copies(1, sources, (key_held, value_held), sems.at[0], cuts, range(cuts))
    pieces += half_copies(0, sources, (key_own, value_own), sems.at[1], cuts, range(key_own.shape[1] // step))
    rates_copy = pltpu.make_async_copy(rates_ref, rates_here, sem)
    rates_copy.start()
    ahead = 3
    for i in range(ahead):
        for c in pieces[i]:
            c.start()
    rates_copy.wait()
    for i in range(cuts):
        for c in pieces[i]:
            c.wait()
        if i + ahead < len(pieces):
            for c in pieces[i + ahead]:
                c.start()
        part = pl.ds(i * step, step)
        end_of_piece(key_held.at[:, part], value_held.at[:, part], rates_here, half_of(1) * width + i * step,
                     signal_ref, sent_ref, ends_ref, end_ref, i * step)
    for p in pieces[cuts:]:
        for c in p:
            c.wait()


def end_shapes(tokens, width):
    part = jax.ShapeDtypeStruct((tokens, width), F32)
    return [jax.ShapeDtypeStruct((ORDER, width), F32), part, part]


def in_hbm(*arrays):
    return [pltpu.with_memory_space_constraint(a, pltpu.HBM) for a in arrays]


def far_end(key, value, rates):
    tokens, channels = key.shape
    width = channels // OWNERS
    return pl.pallas_call(
        far_end_kernel,
        in_specs=[IN_HBM] * 3,
        out_specs=[IN_VMEM] * 5,
        out_shape=end_shapes(tokens, width) + [jax.ShapeDtypeStruct((tokens, width // 2), BF16)] * 2,
        scratch_shapes=[
            pltpu.VMEM((tokens, width), BF16),
            pltpu.VMEM((tokens, width), BF16),
            pltpu.VMEM((SUB * PITCH, LANES), F32),
            pltpu.VMEM((ORDER, channels), F32),
            pltpu.SemaphoreType.DMA((2, 2, 4)),
            pltpu.SemaphoreType.DMA(()),
        ],
        compiler_params=PARAMS,
        cost_estimate=cost(3.4),
        name="far_end",
    )(*in_hbm(key, value, rates))


ENTRIES = 7


def own_end_kernel(key_first, value_first, key_ref, value_ref, rates_ref, end_ref, sent_ref, ends_ref, tables_ref,
                   key_held, value_held, signal_ref, sems):
    tokens, width = key_held.shape
    x, z, _, _ = position()
    first = half_of(0) * width
    cuts = 4
    step = width // cuts
    brought = key_first.shape[1] // step
    pieces = half_copies(0, (key_ref, value_ref), (key_held, value_held), sems, cuts, range(brought, cuts))
    for p in pieces:
        for c in p:
            c.start()

    def table(t, _):
        here = lanes_at(t * LANES)
        rates = rates_ref[:, lanes_at(first + t * LANES)] * float(-tokens)
        tables_ref[0, :, here] = jnp.exp(rates)
        tables_ref[1, :, here] = jnp.exp(rates * 2.0)
        tables_ref[2, :, here] = jnp.exp(rates * (4 * (1 - z)).astype(F32))
        tables_ref[3, :, here] = jnp.exp(rates * (4 * z).astype(F32))
        for k in (1, 2, 3):
            spans = (4 * z + 8 * (k - 1)).astype(F32)
            tables_ref[3 + k, :, here] = jnp.exp(rates * spans) * (x >= k).astype(F32)
        return 0

    lax.fori_loop(0, width // LANES, table, 0)
    for i in range(cuts):
        part = pl.ds(i * step, step)
        if i < brought:
            key, value = key_first, value_first
        else:
            key, value = key_held, value_held
            for c in pieces[i - brought]:
                c.wait()
        end_of_piece(key.at[:, part], value.at[:, part], rates_ref, first + i * step,
                     signal_ref, sent_ref, ends_ref, end_ref, i * step)


def own_end(key_first, value_first, key, value, rates):
    tokens, channels = key.shape
    width = channels // OWNERS
    return pl.pallas_call(
        own_end_kernel,
        in_specs=[IN_VMEM, IN_VMEM, IN_HBM, IN_HBM, IN_VMEM],
        out_specs=[IN_VMEM] * 4,
        out_shape=end_shapes(tokens, width) + [jax.ShapeDtypeStruct((ENTRIES, ORDER, width), F32)],
        scratch_shapes=[
            pltpu.VMEM((tokens, width), BF16),
            pltpu.VMEM((tokens, width), BF16),
            pltpu.VMEM((SUB * PITCH, LANES), F32),
            pltpu.SemaphoreType.DMA((2, 4)),
        ],
        compiler_params=PARAMS,
        cost_estimate=cost(2.7),
        name="own_end",
    )(key_first, value_first, *in_hbm(key, value), rates)


def pair_kernel(own_ref, got_ref, tables_ref, pair_ref):
    _, _, _, odd = position()
    own, got = own_ref[...], got_ref[...]
    earlier, later = jnp.where(odd == 1, got, own), jnp.where(odd == 1, own, got)
    pair_ref[...] = tables_ref[0] * earlier + later


def row_kernel(own_ref, got_ref, tables_ref, row_ref):
    _, _, pair, _ = position()
    own, got = own_ref[...], got_ref[...]
    earlier, later = jnp.where(pair == 1, got, own), jnp.where(pair == 1, own, got)
    row_ref[...] = tables_ref[1] * earlier + later


def plane_kernel(own_ref, got_ref, tables_ref, plane_ref):
    plane_ref[...] = tables_ref[2] * own_ref[...] + tables_ref[3] * got_ref[...]


def states_kernel(own_ref, got_ref, pair_ref, half_ref, p1, p2, p3, tables_ref, mine_ref, other_ref):
    _, z, pair, odd = position()
    head = half_ref[...] * z.astype(F32) + add_up([tables_ref[3 + k] * p[...] for k, p in ((1, p1), (2, p2), (3, p3))])
    earlier = jnp.where(pair == 1, tables_ref[1] * head + pair_ref[...], head)
    later = tables_ref[0] * earlier + jnp.where(odd == 1, got_ref[...], own_ref[...])
    mine_ref[...] = jnp.where(odd == 1, later, earlier)
    other_ref[...] = jnp.where(odd == 1, earlier, later)


def small(kernel, count, *args):
    out = jax.ShapeDtypeStruct(args[0].shape, F32)
    return pl.pallas_call(
        kernel,
        in_specs=[IN_VMEM] * len(args),
        out_specs=[IN_VMEM] * count,
        out_shape=[out] * count,
        compiler_params=PARAMS,
        cost_estimate=cost(0.05),
        name=kernel.__name__,
    )(*args)


def local_kernel(by, sent_ref, ends_ref, gate_ref, rates_ref, residues_ref, skip_ref,
                 mixed_ref, gate_out, start_ref, reach_ref, enter_ref, gate_held, gate_f32, sems):
    tokens, width = mixed_ref.shape
    span = tokens // SUB
    place = lax.broadcasted_iota(jnp.int32, (SUB, LANES), 0).astype(F32)

    def copy(t):
        there = lanes_at(half_of(by) * width + t * LANES)
        return pltpu.make_async_copy(gate_ref.at[:, there], gate_held.at[t], sems.at[t])

    for t in range(width // LANES):
        copy(t).start()

    def tile(t, _):
        lanes = lanes_at(half_of(by) * width + t * LANES)
        here = lanes_at(t * LANES)
        rates = rates_ref[:, lanes]
        residues = residues_ref[:, lanes]
        decay = jnp.exp(-rates)

        taps, term = [], residues
        for k in range(RUN):
            tap = term[:SUB] + term[SUB:]
            for shift in (4, 2, 1):
                tap = tap + pltpu.roll(tap, shift, 0)
            taps.append(tap)
            term = term * decay
        taps[0] = taps[0] + skip_ref[:, lanes]

        run = spread(jnp.exp(rates * float(-RUN)))

        def end(g, n):
            return ends_ref[pl.ds((g * ORDER + n) * SUB, SUB), here]

        state = [(end(0, n) * run[n] + end(1, n)) * run[n] + end(2, n) for n in range(ORDER)]
        for step in (1, 2, 4):
            across = spread(jnp.exp(rates * float(-span * step)))
            state = [s + later(s, step) * a for s, a in zip(state, across)]
        first = spread(residues * decay)
        for n in range(ORDER):
            rows = pl.ds(n * SUB, SUB)
            start_ref[rows, here] = first[n] * later(state[n], 1)
            reach_ref[rows, here] = first[n] * jnp.exp(rates[n : n + 1, :] * (place * float(-span)))
            for g in (0, 1):
                enter_ref[pl.ds((g * ORDER + n) * SUB, SUB), here] = first[n] * end(g, n)

        def group(g, _):
            signal = []
            for i in range(RUN):
                rows = pl.ds(pl.multiple_of((g * RUN + i) * SUB, SUB), SUB)
                signal.append(sent_ref[rows, here])
                mixed_ref[rows, here] = add_up([taps[i - m] * signal[m] for m in range(i + 1)])
            return 0

        lax.fori_loop(0, span // RUN, group, 0)
        return 0

    def gating(t, _):
        here = lanes_at(t * LANES)
        copy(t).wait()
        for s in range(SUB):
            gate_f32[pl.ds(s * PITCH, span), :] = gate_held[t, pl.ds(s * span, span), :].astype(F32)
        for j in range(span):
            rows = pl.ds(j * SUB, SUB)
            gate = gate_f32[pl.ds(j, SUB, stride=PITCH), :]
            mixed_ref[rows, here] = gate * mixed_ref[rows, here]
            gate_out[rows, here] = gate
        return 0

    lax.fori_loop(0, width // LANES, tile, 0)
    lax.fori_loop(0, width // LANES, gating, 0)


def local_part(by, sent, ends, gate, rates, residues, skip):
    tokens, width = sent.shape
    token_part = jax.ShapeDtypeStruct((tokens, width), F32)
    mode_part = jax.ShapeDtypeStruct((ORDER * SUB, width), F32)
    enter_part = jax.ShapeDtypeStruct((2 * ORDER * SUB, width), F32)
    gate = pltpu.with_memory_space_constraint(gate, pltpu.HBM)
    return pl.pallas_call(
        lambda *refs: local_kernel(by, *refs),
        in_specs=[IN_VMEM, IN_VMEM, IN_HBM, IN_VMEM, IN_VMEM, IN_VMEM],
        out_specs=[IN_VMEM] * 5,
        out_shape=[token_part, token_part, mode_part, mode_part, enter_part],
        scratch_shapes=[
            pltpu.VMEM((width // LANES, tokens, LANES), BF16),
            pltpu.VMEM((SUB * PITCH, LANES), F32),
            pltpu.SemaphoreType.DMA((width // LANES,)),
        ],
        compiler_params=PARAMS,
        cost_estimate=cost(2.6),
        name="local_part",
    )(sent, ends, gate, rates, residues, skip)


def mix_kernel(by, last, mixed_ref, gate_ref, start_ref, reach_ref, enter_ref, state_ref, rates_ref, *rest):
    tokens, width = mixed_ref.shape
    span = tokens // SUB
    gated_ref, sums_ref = rest[-2], rest[-1]
    if by == 0:
        sums_ref[...] = jnp.zeros_like(sums_ref)
    else:
        sums_ref[...] = rest[0][...]
    if last:
        power_ref = rest[1]

    def tile(t, _):
        here = lanes_at(t * LANES)
        step = spread(jnp.exp(-rates_ref[:, lanes_at(half_of(by) * width + t * LANES)]))
        state = state_ref[:, here]
        terms = []
        for n in range(ORDER):
            rows = pl.ds(n * SUB, SUB)
            terms.append(start_ref[rows, here] + reach_ref[rows, here] * state[n : n + 1, :])
        for j in range(span):
            if j > 0:
                terms = [a * b for a, b in zip(terms, step)]
            if j > 0 and j % RUN == 0:
                g = j // RUN - 1
                terms = [a + enter_ref[pl.ds((g * ORDER + n) * SUB, SUB), here] for n, a in enumerate(terms)]
            rows = pl.ds(j * SUB, SUB)
            gated = mixed_ref[rows, here] + gate_ref[rows, here] * add_up(terms)
            gated_ref[t, pl.ds(j, SUB, stride=OUT_PITCH), :] = gated
            sums_ref[rows, :] += gated * gated
        return 0

    lax.fori_loop(0, width // LANES, tile, 0)
    if last:
        power_ref[...] = lax.dot_general(
            jnp.ones((SUB, LANES), F32),
            sums_ref[...],
            (((1,), (1,)), ((), ())),
            precision=lax.Precision.HIGHEST,
            preferred_element_type=F32,
        )[0:1, :]


def mix(by, last, part, state, rates, sums):
    tokens, width = part[0].shape
    out_sums = jax.ShapeDtypeStruct((tokens, LANES), F32)
    gated = jax.ShapeDtypeStruct((width // LANES, SUB * OUT_PITCH, LANES), F32)
    args = [*part, state, rates] + ([] if sums is None else [sums])
    if last:
        outs, scratch = [jax.ShapeDtypeStruct((1, tokens), F32), gated], [pltpu.VMEM((tokens, LANES), F32)]
    else:
        outs, scratch = [gated, out_sums], []
    return pl.pallas_call(
        lambda *refs: mix_kernel(by, last, *refs),
        in_specs=[IN_VMEM] * len(args),
        out_specs=[IN_VMEM] * 2,
        out_shape=outs,
        scratch_shapes=scratch,
        compiler_params=PARAMS,
        cost_estimate=cost(2.1),
        name="mix",
    )(*args)


def norm_kernel(g0, g1, gain_ref, p0_ref, p1_ref, p2_ref, p3_ref, out_ref, runs_ref, scale_ref, held, sems):
    tiles, tokens = g0.shape[0], scale_ref.shape[0]
    width = tiles * LANES
    span = tokens // SUB
    total = (p0_ref[...] + p1_ref[...]) + (p2_ref[...] + p3_ref[...])
    first = (lax.broadcasted_iota(jnp.int32, (SUB, LANES), 0) == 0).astype(F32)
    power = lax.dot_general(
        jnp.broadcast_to(total, (SUB, tokens)),
        first,
        (((0,), (0,)), ((), ())),
        precision=lax.Precision.HIGHEST,
        preferred_element_type=F32,
    )
    runs_ref[...] = lax.rsqrt(power * (1.0 / D) + 1e-6)
    for i in range(span):
        scale_ref[pl.ds(i, SUB, stride=span), :] = runs_ref[pl.ds(i * SUB, SUB), :]

    copies = []
    cuts = sems.shape[1]
    step = width // cuts
    for by, gated_ref in enumerate((g0, g1)):
        first = half_of(by) * width

        def tile(t, _):
            here = lanes_at(t * LANES)
            gain = gain_ref[:, lanes_at(first + t * LANES)]
            for s in range(SUB):
                rows = pl.ds(s * span, span)
                gated = gated_ref[t, pl.ds(s * OUT_PITCH, span), :]
                held[by, rows, here] = (gated * scale_ref[rows, :] * gain).astype(BF16)
            return 0

        for cut in range(cuts):
            lax.fori_loop(cut * tiles // cuts, (cut + 1) * tiles // cuts, tile, 0)
            copy = pltpu.make_async_copy(
                held.at[by, :, pl.ds(cut * step, step)],
                out_ref.at[:, pl.ds(pl.multiple_of(first + cut * step, step), step)],
                sems.at[by, cut],
            )
            copy.start()
            copies.append(copy)
    for copy in copies:
        copy.wait()


def norm(gated, gain, powers):
    tiles, tokens = gated[0].shape[0], powers[0].shape[1]
    width = tiles * LANES
    channels = width * OWNERS
    return pl.pallas_call(
        norm_kernel,
        in_specs=[IN_VMEM] * 7,
        out_specs=IN_HBM,
        out_shape=jax.ShapeDtypeStruct((tokens, channels), BF16),
        scratch_shapes=[
            pltpu.VMEM((tokens, LANES), F32),
            pltpu.VMEM((tokens, LANES), F32),
            pltpu.VMEM((OWNERS, tokens, width), BF16),
            pltpu.SemaphoreType.DMA((OWNERS, 4)),
        ],
        compiler_params=PARAMS,
        cost_estimate=cost(1.7),
        name="norm",
    )(*gated, gain, *powers)


def with_partner(x, by):
    return lax.ppermute(x, "seq", [(i, i ^ by) for i in range(32)])


def over_x(x, by):
    return lax.ppermute(x, "seq", [(i, (i + 8 * by) % 32) for i in range(32)])


def over_ch(x, by):
    return lax.ppermute(x, "ch", [(i, (i + by) % 4) for i in range(4)])


def body(gate, key, value, rates, residues, skip_gain, norm_gain):
    skip = skip_gain[None, :]
    tie = lax.optimization_barrier

    far, far_sent, far_ends, *first = far_end(key, value, rates)
    far, rates0 = tie((far, rates))
    got = with_partner(far, 1)
    own, own_sent, own_ends, tables = own_end(*first, key, value, rates0)
    (pair,) = small(pair_kernel, 1, own, got, tables)

    pair, rates1 = tie((pair, rates))
    other_pair = with_partner(pair, 3)
    far_part = local_part(1, far_sent, far_ends, gate, rates1, residues, skip)
    other_pair, *far_part = tie((other_pair, *far_part))
    (row,) = small(row_kernel, 1, pair, other_pair, tables)

    row, rates2 = tie((row, rates))
    other_row = with_partner(row, 4)
    own_part = local_part(0, own_sent, own_ends, gate, rates2, residues, skip)
    other_row, *own_part = tie((other_row, *own_part))
    (plane,) = small(plane_kernel, 1, row, other_row, tables)

    planes = [over_x(plane, k) for k in (1, 2, 3)]
    mine, theirs = small(states_kernel, 2, own, got, other_pair, other_row, *planes, tables)

    theirs = with_partner(theirs, 1)
    own_gated, sums = mix(0, False, own_part, mine, rates, None)
    power, far_gated = mix(1, True, far_part, theirs, rates, sums)
    powers = [power] + [over_ch(power, k) for k in (1, 2, 3)]
    return norm([own_gated, far_gated], norm_gain[None, :], powers)


def solution(mesh):
    placed = (
        P("seq", "ch"),
        P("seq", "ch"),
        P("seq", "ch"),
        P(None, "ch"),
        P(None, "ch"),
        P("ch"),
        P("ch"),
    )
    return jax.shard_map(
        body, mesh=mesh, in_specs=placed, out_specs=P("seq", "ch"), check_vma=False
    )
```

```python
import jax
import jax.numpy as jnp
from jax import lax
from jax.experimental import pallas as pl
from jax.experimental.pallas import tpu as pltpu
from jax.sharding import PartitionSpec as P

D = 8192
ORDER = 16
LANES = 128
SUB = 8
RUN = 16
PITCH = 52
OUT_PITCH = 50
OWNERS = 2
F32 = jnp.float32
BF16 = jnp.bfloat16

IN_HBM = pl.BlockSpec(memory_space=pltpu.HBM)
IN_VMEM = pl.BlockSpec(memory_space=pltpu.VMEM)
PARAMS = pltpu.CompilerParams(vmem_limit_bytes=24 << 20)


def cost(us):
    return pl.CostEstimate(flops=int(us * 1.15e9), bytes_accessed=int(us * 3.69e6), transcendentals=0)


def spread(table):
    return [jnp.broadcast_to(table[n : n + 1, :], (SUB, LANES)) for n in range(ORDER)]


def add_up(terms):
    terms = list(terms)
    while len(terms) > 1:
        terms = [a + b for a, b in zip(terms[::2], terms[1::2])] + terms[len(terms) & ~1 :]
    return terms[0]


def position():
    place = lax.axis_index("seq")
    return lax.div(place, 8), lax.rem(lax.div(place, 4), 2), lax.rem(lax.div(place, 2), 2), lax.rem(place, 2)


def half_of(by):
    _, _, pair, odd = position()
    return lax.rem(pair + odd + by, 2)


def lanes_at(first):
    return pl.ds(pl.multiple_of(first, LANES), LANES)


def later(x, by):
    place = lax.broadcasted_iota(jnp.int32, (SUB, LANES), 0)
    return jnp.where(place >= by, pltpu.roll(x, by, 0), 0.0)


def end_of_tile(span, signal_ref, rates, sent_ref, ends_ref, here):
    one = spread(jnp.exp(-rates))
    run = spread(jnp.exp(rates * float(-RUN)))
    total = None
    for g in range(span // RUN):
        acc = None
        for i in range(RUN):
            j = g * RUN + i
            signal = signal_ref[pl.ds(j, SUB, stride=PITCH), :]
            sent_ref[pl.ds(j * SUB, SUB), here] = signal
            acc = [signal] * ORDER if acc is None else [a * o + signal for a, o in zip(acc, one)]
        for n in range(ORDER):
            ends_ref[pl.ds((g * ORDER + n) * SUB, SUB), here] = acc[n]
        total = acc if total is None else [t * r + a for t, r, a in zip(total, run, acc)]
    for by in (1, 2, 4):
        across = spread(jnp.exp(rates * float(-span * by)))
        total = [t + pltpu.roll(t, by, 0) * a for t, a in zip(total, across)]
    return [t[SUB - 1 :, :] for t in total]


def end_of_piece(key_ref, value_ref, rates_ref, first, signal_ref, sent_ref, ends_ref, end_ref, at):
    span = key_ref.shape[0] // SUB

    def tile(t, _):
        there, here = lanes_at(t * LANES), lanes_at(at + t * LANES)
        for s in range(SUB):
            rows = pl.ds(s * span, span)
            signal_ref[pl.ds(s * PITCH, span), :] = key_ref[rows, there].astype(F32) * value_ref[rows, there].astype(F32)
        ends = end_of_tile(span, signal_ref, rates_ref[:, lanes_at(first + t * LANES)], sent_ref, ends_ref, here)
        for n in range(ORDER):
            end_ref[n : n + 1, here] = ends[n]
        return 0

    lax.fori_loop(0, key_ref.shape[1] // LANES, tile, 0)


def half_copies(by, sources, targets, sems, cuts, which):
    width = sources[0].shape[1] // OWNERS
    step = width // cuts
    return [
        [
            pltpu.make_async_copy(
                a.at[:, pl.ds(pl.multiple_of(half_of(by) * width + j * step, step), step)],
                b.at[:, pl.ds(j * step, step)],
                sems.at[s, j],
            )
            for s, (a, b) in enumerate(zip(sources, targets))
        ]
        for j in which
    ]


def far_end_kernel(key_ref, value_ref, rates_ref, end_ref, sent_ref, ends_ref, key_own, value_own,
                   key_held, value_held, signal_ref, rates_here, sems, sem):
    width = key_held.shape[1]
    cuts = 4
    step = width // cuts
    sources = (key_ref, value_ref)
    pieces = half_copies(1, sources, (key_held, value_held), sems.at[0], cuts, range(cuts))
    pieces += half_copies(0, sources, (key_own, value_own), sems.at[1], cuts, range(key_own.shape[1] // step))
    rates_copy = pltpu.make_async_copy(rates_ref, rates_here, sem)
    rates_copy.start()
    ahead = 3
    for i in range(ahead):
        for c in pieces[i]:
            c.start()
    rates_copy.wait()
    for i in range(cuts):
        for c in pieces[i]:
            c.wait()
        if i + ahead < len(pieces):
            for c in pieces[i + ahead]:
                c.start()
        part = pl.ds(i * step, step)
        end_of_piece(key_held.at[:, part], value_held.at[:, part], rates_here, half_of(1) * width + i * step,
                     signal_ref, sent_ref, ends_ref, end_ref, i * step)
    for p in pieces[cuts:]:
        for c in p:
            c.wait()


def end_shapes(tokens, width):
    part = jax.ShapeDtypeStruct((tokens, width), F32)
    return [jax.ShapeDtypeStruct((ORDER, width), F32), part, part]


def in_hbm(*arrays):
    return [pltpu.with_memory_space_constraint(a, pltpu.HBM) for a in arrays]


def far_end(key, value, rates):
    tokens, channels = key.shape
    width = channels // OWNERS
    return pl.pallas_call(
        far_end_kernel,
        in_specs=[IN_HBM] * 3,
        out_specs=[IN_VMEM] * 5,
        out_shape=end_shapes(tokens, width) + [jax.ShapeDtypeStruct((tokens, width // 2), BF16)] * 2,
        scratch_shapes=[
            pltpu.VMEM((tokens, width), BF16),
            pltpu.VMEM((tokens, width), BF16),
            pltpu.VMEM((SUB * PITCH, LANES), F32),
            pltpu.VMEM((ORDER, channels), F32),
            pltpu.SemaphoreType.DMA((2, 2, 4)),
            pltpu.SemaphoreType.DMA(()),
        ],
        compiler_params=PARAMS,
        cost_estimate=cost(3.4),
        name="far_end",
    )(*in_hbm(key, value, rates))


ENTRIES = 7


def own_end_kernel(key_first, value_first, key_ref, value_ref, rates_ref, end_ref, sent_ref, ends_ref, tables_ref,
                   key_held, value_held, signal_ref, sems):
    tokens, width = key_held.shape
    x, z, _, _ = position()
    first = half_of(0) * width
    cuts = 4
    step = width // cuts
    brought = key_first.shape[1] // step
    pieces = half_copies(0, (key_ref, value_ref), (key_held, value_held), sems, cuts, range(brought, cuts))
    for p in pieces:
        for c in p:
            c.start()

    def table(t, _):
        here = lanes_at(t * LANES)
        rates = rates_ref[:, lanes_at(first + t * LANES)] * float(-tokens)
        tables_ref[0, :, here] = jnp.exp(rates)
        tables_ref[1, :, here] = jnp.exp(rates * 2.0)
        tables_ref[2, :, here] = jnp.exp(rates * (4 * (1 - z)).astype(F32))
        tables_ref[3, :, here] = jnp.exp(rates * (4 * z).astype(F32))
        for k in (1, 2, 3):
            spans = (4 * z + 8 * (k - 1)).astype(F32)
            tables_ref[3 + k, :, here] = jnp.exp(rates * spans) * (x >= k).astype(F32)
        return 0

    lax.fori_loop(0, width // LANES, table, 0)
    for i in range(cuts):
        part = pl.ds(i * step, step)
        if i < brought:
            key, value = key_first, value_first
        else:
            key, value = key_held, value_held
            for c in pieces[i - brought]:
                c.wait()
        end_of_piece(key.at[:, part], value.at[:, part], rates_ref, first + i * step,
                     signal_ref, sent_ref, ends_ref, end_ref, i * step)


def own_end(key_first, value_first, key, value, rates):
    tokens, channels = key.shape
    width = channels // OWNERS
    return pl.pallas_call(
        own_end_kernel,
        in_specs=[IN_VMEM, IN_VMEM, IN_HBM, IN_HBM, IN_VMEM],
        out_specs=[IN_VMEM] * 4,
        out_shape=end_shapes(tokens, width) + [jax.ShapeDtypeStruct((ENTRIES, ORDER, width), F32)],
        scratch_shapes=[
            pltpu.VMEM((tokens, width), BF16),
            pltpu.VMEM((tokens, width), BF16),
            pltpu.VMEM((SUB * PITCH, LANES), F32),
            pltpu.SemaphoreType.DMA((2, 4)),
        ],
        compiler_params=PARAMS,
        cost_estimate=cost(2.7),
        name="own_end",
    )(key_first, value_first, *in_hbm(key, value), rates)


def pair_kernel(own_ref, got_ref, tables_ref, pair_ref):
    _, _, _, odd = position()
    own, got = own_ref[...], got_ref[...]
    earlier, later = jnp.where(odd == 1, got, own), jnp.where(odd == 1, own, got)
    pair_ref[...] = tables_ref[0] * earlier + later


def row_kernel(own_ref, got_ref, tables_ref, row_ref):
    _, _, pair, _ = position()
    own, got = own_ref[...], got_ref[...]
    earlier, later = jnp.where(pair == 1, got, own), jnp.where(pair == 1, own, got)
    row_ref[...] = tables_ref[1] * earlier + later


def plane_kernel(own_ref, got_ref, tables_ref, plane_ref):
    plane_ref[...] = tables_ref[2] * own_ref[...] + tables_ref[3] * got_ref[...]


def states_kernel(own_ref, got_ref, pair_ref, half_ref, p1, p2, p3, tables_ref, mine_ref, other_ref):
    _, z, pair, odd = position()
    head = half_ref[...] * z.astype(F32) + add_up([tables_ref[3 + k] * p[...] for k, p in ((1, p1), (2, p2), (3, p3))])
    earlier = jnp.where(pair == 1, tables_ref[1] * head + pair_ref[...], head)
    later = tables_ref[0] * earlier + jnp.where(odd == 1, got_ref[...], own_ref[...])
    mine_ref[...] = jnp.where(odd == 1, later, earlier)
    other_ref[...] = jnp.where(odd == 1, earlier, later)


def small(kernel, count, *args):
    out = jax.ShapeDtypeStruct(args[0].shape, F32)
    return pl.pallas_call(
        kernel,
        in_specs=[IN_VMEM] * len(args),
        out_specs=[IN_VMEM] * count,
        out_shape=[out] * count,
        compiler_params=PARAMS,
        cost_estimate=cost(0.05),
        name=kernel.__name__,
    )(*args)


def local_kernel(by, sent_ref, ends_ref, gate_ref, rates_ref, residues_ref, skip_ref,
                 mixed_ref, gate_out, start_ref, reach_ref, enter_ref, gate_held, gate_f32, sems):
    tokens, width = mixed_ref.shape
    span = tokens // SUB
    place = lax.broadcasted_iota(jnp.int32, (SUB, LANES), 0).astype(F32)

    def copy(t):
        there = lanes_at(half_of(by) * width + t * LANES)
        return pltpu.make_async_copy(gate_ref.at[:, there], gate_held.at[t], sems.at[t])

    for t in range(width // LANES):
        copy(t).start()

    def tile(t, _):
        lanes = lanes_at(half_of(by) * width + t * LANES)
        here = lanes_at(t * LANES)
        rates = rates_ref[:, lanes]
        residues = residues_ref[:, lanes]
        decay = jnp.exp(-rates)

        taps, term = [], residues
        for k in range(RUN):
            tap = term[:SUB] + term[SUB:]
            for shift in (4, 2, 1):
                tap = tap + pltpu.roll(tap, shift, 0)
            taps.append(tap)
            term = term * decay
        taps[0] = taps[0] + skip_ref[:, lanes]

        run = spread(jnp.exp(rates * float(-RUN)))

        def end(g, n):
            return ends_ref[pl.ds((g * ORDER + n) * SUB, SUB), here]

        state = [(end(0, n) * run[n] + end(1, n)) * run[n] + end(2, n) for n in range(ORDER)]
        for step in (1, 2, 4):
            across = spread(jnp.exp(rates * float(-span * step)))
            state = [s + later(s, step) * a for s, a in zip(state, across)]
        first = spread(residues * decay)
        for n in range(ORDER):
            rows = pl.ds(n * SUB, SUB)
            start_ref[rows, here] = first[n] * later(state[n], 1)
            reach_ref[rows, here] = first[n] * jnp.exp(rates[n : n + 1, :] * (place * float(-span)))
            for g in (0, 1):
                enter_ref[pl.ds((g * ORDER + n) * SUB, SUB), here] = first[n] * end(g, n)

        def group(g, _):
            signal = []
            for i in range(RUN):
                rows = pl.ds(pl.multiple_of((g * RUN + i) * SUB, SUB), SUB)
                signal.append(sent_ref[rows, here])
                mixed_ref[rows, here] = add_up([taps[i - m] * signal[m] for m in range(i + 1)])
            return 0

        lax.fori_loop(0, span // RUN, group, 0)
        return 0

    def gating(t, _):
        here = lanes_at(t * LANES)
        copy(t).wait()
        for s in range(SUB):
            gate_f32[pl.ds(s * PITCH, span), :] = gate_held[t, pl.ds(s * span, span), :].astype(F32)
        for j in range(span):
            rows = pl.ds(j * SUB, SUB)
            gate = gate_f32[pl.ds(j, SUB, stride=PITCH), :]
            mixed_ref[rows, here] = gate * mixed_ref[rows, here]
            gate_out[rows, here] = gate
        return 0

    lax.fori_loop(0, width // LANES, tile, 0)
    lax.fori_loop(0, width // LANES, gating, 0)


def local_part(by, sent, ends, gate, rates, residues, skip):
    tokens, width = sent.shape
    token_part = jax.ShapeDtypeStruct((tokens, width), F32)
    mode_part = jax.ShapeDtypeStruct((ORDER * SUB, width), F32)
    enter_part = jax.ShapeDtypeStruct((2 * ORDER * SUB, width), F32)
    gate = pltpu.with_memory_space_constraint(gate, pltpu.HBM)
    return pl.pallas_call(
        lambda *refs: local_kernel(by, *refs),
        in_specs=[IN_VMEM, IN_VMEM, IN_HBM, IN_VMEM, IN_VMEM, IN_VMEM],
        out_specs=[IN_VMEM] * 5,
        out_shape=[token_part, token_part, mode_part, mode_part, enter_part],
        scratch_shapes=[
            pltpu.VMEM((width // LANES, tokens, LANES), BF16),
            pltpu.VMEM((SUB * PITCH, LANES), F32),
            pltpu.SemaphoreType.DMA((width // LANES,)),
        ],
        compiler_params=PARAMS,
        cost_estimate=cost(2.6),
        name="local_part",
    )(sent, ends, gate, rates, residues, skip)


def mix_kernel(by, last, mixed_ref, gate_ref, start_ref, reach_ref, enter_ref, state_ref, rates_ref, *rest):
    tokens, width = mixed_ref.shape
    span = tokens // SUB
    gated_ref, sums_ref = rest[-2], rest[-1]
    if by == 0:
        sums_ref[...] = jnp.zeros_like(sums_ref)
    else:
        sums_ref[...] = rest[0][...]
    if last:
        power_ref = rest[1]

    def tile(t, _):
        here = lanes_at(t * LANES)
        step = spread(jnp.exp(-rates_ref[:, lanes_at(half_of(by) * width + t * LANES)]))
        state = state_ref[:, here]
        terms = []
        for n in range(ORDER):
            rows = pl.ds(n * SUB, SUB)
            terms.append(start_ref[rows, here] + reach_ref[rows, here] * state[n : n + 1, :])
        for j in range(span):
            if j > 0:
                terms = [a * b for a, b in zip(terms, step)]
            if j > 0 and j % RUN == 0:
                g = j // RUN - 1
                terms = [a + enter_ref[pl.ds((g * ORDER + n) * SUB, SUB), here] for n, a in enumerate(terms)]
            rows = pl.ds(j * SUB, SUB)
            gated = mixed_ref[rows, here] + gate_ref[rows, here] * add_up(terms)
            gated_ref[t, pl.ds(j, SUB, stride=OUT_PITCH), :] = gated
            sums_ref[rows, :] += gated * gated
        return 0

    lax.fori_loop(0, width // LANES, tile, 0)
    if last:
        for block in range(tokens // LANES):
            rows = pl.ds(block * LANES, LANES)
            power_ref[:, rows] = jnp.sum(jnp.transpose(sums_ref[rows, :]), axis=0, keepdims=True)


def mix(by, last, part, state, rates, sums):
    tokens, width = part[0].shape
    out_sums = jax.ShapeDtypeStruct((tokens, LANES), F32)
    gated = jax.ShapeDtypeStruct((width // LANES, SUB * OUT_PITCH, LANES), F32)
    args = [*part, state, rates] + ([] if sums is None else [sums])
    if last:
        outs, scratch = [jax.ShapeDtypeStruct((1, tokens), F32), gated], [pltpu.VMEM((tokens, LANES), F32)]
    else:
        outs, scratch = [gated, out_sums], []
    return pl.pallas_call(
        lambda *refs: mix_kernel(by, last, *refs),
        in_specs=[IN_VMEM] * len(args),
        out_specs=[IN_VMEM] * 2,
        out_shape=outs,
        scratch_shapes=scratch,
        compiler_params=PARAMS,
        cost_estimate=cost(2.1),
        name="mix",
    )(*args)


def norm_kernel(g0, g1, gain_ref, p0_ref, p1_ref, p2_ref, p3_ref, out_ref, runs_ref, scale_ref, held, sems):
    tiles, tokens = g0.shape[0], scale_ref.shape[0]
    width = tiles * LANES
    span = tokens // SUB
    total = (p0_ref[...] + p1_ref[...]) + (p2_ref[...] + p3_ref[...])
    power = jnp.transpose(jnp.broadcast_to(total, (LANES, tokens)))
    runs_ref[...] = lax.rsqrt(power * (1.0 / D) + 1e-6)
    for i in range(span):
        scale_ref[pl.ds(i, SUB, stride=span), :] = runs_ref[pl.ds(i * SUB, SUB), :]

    copies = []
    cuts = sems.shape[1]
    step = width // cuts
    for by, gated_ref in enumerate((g0, g1)):
        first = half_of(by) * width

        def tile(t, _):
            here = lanes_at(t * LANES)
            gain = gain_ref[:, lanes_at(first + t * LANES)]
            for s in range(SUB):
                rows = pl.ds(s * span, span)
                gated = gated_ref[t, pl.ds(s * OUT_PITCH, span), :]
                held[by, rows, here] = (gated * scale_ref[rows, :] * gain).astype(BF16)
            return 0

        for cut in range(cuts):
            lax.fori_loop(cut * tiles // cuts, (cut + 1) * tiles // cuts, tile, 0)
            copy = pltpu.make_async_copy(
                held.at[by, :, pl.ds(cut * step, step)],
                out_ref.at[:, pl.ds(pl.multiple_of(first + cut * step, step), step)],
                sems.at[by, cut],
            )
            copy.start()
            copies.append(copy)
    for copy in copies:
        copy.wait()


def norm(gated, gain, powers):
    tiles, tokens = gated[0].shape[0], powers[0].shape[1]
    width = tiles * LANES
    channels = width * OWNERS
    return pl.pallas_call(
        norm_kernel,
        in_specs=[IN_VMEM] * 7,
        out_specs=IN_HBM,
        out_shape=jax.ShapeDtypeStruct((tokens, channels), BF16),
        scratch_shapes=[
            pltpu.VMEM((tokens, LANES), F32),
            pltpu.VMEM((tokens, LANES), F32),
            pltpu.VMEM((OWNERS, tokens, width), BF16),
            pltpu.SemaphoreType.DMA((OWNERS, 8)),
        ],
        compiler_params=PARAMS,
        cost_estimate=cost(1.7),
        name="norm",
    )(*gated, gain, *powers)


def with_partner(x, by):
    return lax.ppermute(x, "seq", [(i, i ^ by) for i in range(32)])


def over_x(x, by):
    return lax.ppermute(x, "seq", [(i, (i + 8 * by) % 32) for i in range(32)])


def over_ch(x, by):
    return lax.ppermute(x, "ch", [(i, i ^ by) for i in range(4)])


def body(gate, key, value, rates, residues, skip_gain, norm_gain):
    skip = skip_gain[None, :]
    tie = lax.optimization_barrier

    far, far_sent, far_ends, *first = far_end(key, value, rates)
    far, rates0 = tie((far, rates))
    got = with_partner(far, 1)
    own, own_sent, own_ends, tables = own_end(*first, key, value, rates0)
    (pair,) = small(pair_kernel, 1, own, got, tables)

    pair, rates1 = tie((pair, rates))
    other_pair = with_partner(pair, 3)
    far_part = local_part(1, far_sent, far_ends, gate, rates1, residues, skip)
    other_pair, *far_part = tie((other_pair, *far_part))
    (row,) = small(row_kernel, 1, pair, other_pair, tables)

    row, rates2 = tie((row, rates))
    other_row = with_partner(row, 4)
    own_part = local_part(0, own_sent, own_ends, gate, rates2, residues, skip)
    other_row, *own_part = tie((other_row, *own_part))
    (plane,) = small(plane_kernel, 1, row, other_row, tables)

    planes = [over_x(plane, k) for k in (1, 2, 3)]
    mine, theirs = small(states_kernel, 2, own, got, other_pair, other_row, *planes, tables)

    theirs = with_partner(theirs, 1)
    own_gated, sums = mix(0, False, own_part, mine, rates, None)
    power, far_gated = mix(1, True, far_part, theirs, rates, sums)
    powers = [power] + [over_ch(power, k) for k in (1, 2, 3)]
    return norm([own_gated, far_gated], norm_gain[None, :], powers)


def solution(mesh):
    placed = (
        P("seq", "ch"),
        P("seq", "ch"),
        P("seq", "ch"),
        P(None, "ch"),
        P(None, "ch"),
        P("ch"),
        P("ch"),
    )
    return jax.shard_map(
        body, mesh=mesh, in_specs=placed, out_specs=P("seq", "ch"), check_vma=False
    )
```

```python
import jax
import jax.numpy as jnp
from jax import lax
from jax.experimental import pallas as pl
from jax.experimental.pallas import tpu as pltpu
from jax.sharding import PartitionSpec as P

D = 8192
ORDER = 16
LANES = 128
SUB = 8
RUN = 16
PITCH = 52
OUT_PITCH = 50
OWNERS = 2
F32 = jnp.float32
BF16 = jnp.bfloat16

IN_HBM = pl.BlockSpec(memory_space=pltpu.HBM)
IN_VMEM = pl.BlockSpec(memory_space=pltpu.VMEM)
PARAMS = pltpu.CompilerParams(vmem_limit_bytes=24 << 20)


def cost(us):
    return pl.CostEstimate(flops=int(us * 1.15e9), bytes_accessed=int(us * 3.69e6), transcendentals=0)


def spread(table):
    return [jnp.broadcast_to(table[n : n + 1, :], (SUB, LANES)) for n in range(ORDER)]


def add_up(terms):
    terms = list(terms)
    while len(terms) > 1:
        terms = [a + b for a, b in zip(terms[::2], terms[1::2])] + terms[len(terms) & ~1 :]
    return terms[0]


def position():
    place = lax.axis_index("seq")
    return lax.div(place, 8), lax.rem(lax.div(place, 4), 2), lax.rem(lax.div(place, 2), 2), lax.rem(place, 2)


def half_of(by):
    _, _, pair, odd = position()
    return lax.rem(pair + odd + by, 2)


def lanes_at(first):
    return pl.ds(pl.multiple_of(first, LANES), LANES)


def later(x, by):
    place = lax.broadcasted_iota(jnp.int32, (SUB, LANES), 0)
    return jnp.where(place >= by, pltpu.roll(x, by, 0), 0.0)


def fill_decays(span, rates_ref, first, decays_ref):
    def tile(t, _):
        rates = rates_ref[:, lanes_at(first + t * LANES)]
        for i, length in enumerate((1, RUN, span, 2 * span, 4 * span)):
            decays_ref[i, :, lanes_at(t * LANES)] = jnp.exp(rates * float(-length))
        return 0

    lax.fori_loop(0, decays_ref.shape[2] // LANES, tile, 0)


def end_of_tile(span, signal_ref, decays_ref, sent_ref, ends_ref, here):
    one = spread(decays_ref[0, :, here])
    run = spread(decays_ref[1, :, here])
    total = None
    for g in range(span // RUN):
        acc = None
        for i in range(RUN):
            j = g * RUN + i
            signal = signal_ref[pl.ds(j, SUB, stride=PITCH), :]
            sent_ref[pl.ds(j * SUB, SUB), here] = signal
            acc = [signal] * ORDER if acc is None else [a * o + signal for a, o in zip(acc, one)]
        for n in range(ORDER):
            ends_ref[pl.ds((g * ORDER + n) * SUB, SUB), here] = acc[n]
        total = acc if total is None else [t * r + a for t, r, a in zip(total, run, acc)]
    for i, by in enumerate((1, 2, 4)):
        across = spread(decays_ref[2 + i, :, here])
        total = [t + pltpu.roll(t, by, 0) * a for t, a in zip(total, across)]
    return [t[SUB - 1 :, :] for t in total]


def end_of_piece(key_ref, value_ref, decays_ref, signal_ref, sent_ref, ends_ref, end_ref, at):
    span = key_ref.shape[0] // SUB

    def tile(t, _):
        there, here = lanes_at(t * LANES), lanes_at(at + t * LANES)
        for s in range(SUB):
            rows = pl.ds(s * span, span)
            signal_ref[pl.ds(s * PITCH, span), :] = key_ref[rows, there].astype(F32) * value_ref[rows, there].astype(F32)
        ends = end_of_tile(span, signal_ref, decays_ref, sent_ref, ends_ref, here)
        for n in range(ORDER):
            end_ref[n : n + 1, here] = ends[n]
        return 0

    lax.fori_loop(0, key_ref.shape[1] // LANES, tile, 0)


def half_copies(by, sources, targets, sems, cuts, which):
    width = sources[0].shape[1] // OWNERS
    step = width // cuts
    return [
        [
            pltpu.make_async_copy(
                a.at[:, pl.ds(pl.multiple_of(half_of(by) * width + j * step, step), step)],
                b.at[:, pl.ds(j * step, step)],
                sems.at[s, j],
            )
            for s, (a, b) in enumerate(zip(sources, targets))
        ]
        for j in which
    ]


def far_end_kernel(key_ref, value_ref, rates_ref, end_ref, sent_ref, ends_ref, key_own, value_own,
                   key_held, value_held, signal_ref, rates_here, decays_ref, sems, sem):
    width = key_held.shape[1]
    cuts = 4
    step = width // cuts
    sources = (key_ref, value_ref)
    pieces = half_copies(1, sources, (key_held, value_held), sems.at[0], cuts, range(cuts))
    pieces += half_copies(0, sources, (key_own, value_own), sems.at[1], cuts, range(key_own.shape[1] // step))
    rates_copy = pltpu.make_async_copy(rates_ref, rates_here, sem)
    rates_copy.start()
    ahead = 3
    for i in range(ahead):
        for c in pieces[i]:
            c.start()
    rates_copy.wait()
    fill_decays(key_ref.shape[0] // SUB, rates_here, half_of(1) * width, decays_ref)
    for i in range(cuts):
        for c in pieces[i]:
            c.wait()
        if i + ahead < len(pieces):
            for c in pieces[i + ahead]:
                c.start()
        part = pl.ds(i * step, step)
        end_of_piece(key_held.at[:, part], value_held.at[:, part], decays_ref,
                     signal_ref, sent_ref, ends_ref, end_ref, i * step)
    for p in pieces[cuts:]:
        for c in p:
            c.wait()


def end_shapes(tokens, width):
    part = jax.ShapeDtypeStruct((tokens, width), F32)
    return [jax.ShapeDtypeStruct((ORDER, width), F32), part, part]


def in_hbm(*arrays):
    return [pltpu.with_memory_space_constraint(a, pltpu.HBM) for a in arrays]


def far_end(key, value, rates):
    tokens, channels = key.shape
    width = channels // OWNERS
    return pl.pallas_call(
        far_end_kernel,
        in_specs=[IN_HBM] * 3,
        out_specs=[IN_VMEM] * 5,
        out_shape=end_shapes(tokens, width) + [jax.ShapeDtypeStruct((tokens, width // 2), BF16)] * 2,
        scratch_shapes=[
            pltpu.VMEM((tokens, width), BF16),
            pltpu.VMEM((tokens, width), BF16),
            pltpu.VMEM((SUB * PITCH, LANES), F32),
            pltpu.VMEM((ORDER, channels), F32),
            pltpu.VMEM((5, ORDER, width), F32),
            pltpu.SemaphoreType.DMA((2, 2, 4)),
            pltpu.SemaphoreType.DMA(()),
        ],
        compiler_params=PARAMS,
        cost_estimate=cost(3.4),
        name="far_end",
    )(*in_hbm(key, value, rates))


ENTRIES = 7


def own_end_kernel(key_first, value_first, key_ref, value_ref, rates_ref, end_ref, sent_ref, ends_ref, tables_ref,
                   key_held, value_held, signal_ref, decays_ref, sems):
    tokens, width = key_held.shape
    x, z, _, _ = position()
    first = half_of(0) * width
    cuts = 4
    step = width // cuts
    brought = key_first.shape[1] // step
    pieces = half_copies(0, (key_ref, value_ref), (key_held, value_held), sems, cuts, range(brought, cuts))
    for p in pieces:
        for c in p:
            c.start()

    def table(t, _):
        here = lanes_at(t * LANES)
        rates = rates_ref[:, lanes_at(first + t * LANES)] * float(-tokens)
        tables_ref[0, :, here] = jnp.exp(rates)
        tables_ref[1, :, here] = jnp.exp(rates * 2.0)
        tables_ref[2, :, here] = jnp.exp(rates * (4 * (1 - z)).astype(F32))
        tables_ref[3, :, here] = jnp.exp(rates * (4 * z).astype(F32))
        for k in (1, 2, 3):
            spans = (4 * z + 8 * (k - 1)).astype(F32)
            tables_ref[3 + k, :, here] = jnp.exp(rates * spans) * (x >= k).astype(F32)
        return 0

    lax.fori_loop(0, width // LANES, table, 0)
    fill_decays(tokens // SUB, rates_ref, first, decays_ref)
    for i in range(cuts):
        part = pl.ds(i * step, step)
        if i < brought:
            key, value = key_first, value_first
        else:
            key, value = key_held, value_held
            for c in pieces[i - brought]:
                c.wait()
        end_of_piece(key.at[:, part], value.at[:, part], decays_ref,
                     signal_ref, sent_ref, ends_ref, end_ref, i * step)


def own_end(key_first, value_first, key, value, rates):
    tokens, channels = key.shape
    width = channels // OWNERS
    return pl.pallas_call(
        own_end_kernel,
        in_specs=[IN_VMEM, IN_VMEM, IN_HBM, IN_HBM, IN_VMEM],
        out_specs=[IN_VMEM] * 4,
        out_shape=end_shapes(tokens, width) + [jax.ShapeDtypeStruct((ENTRIES, ORDER, width), F32)],
        scratch_shapes=[
            pltpu.VMEM((tokens, width), BF16),
            pltpu.VMEM((tokens, width), BF16),
            pltpu.VMEM((SUB * PITCH, LANES), F32),
            pltpu.VMEM((5, ORDER, width), F32),
            pltpu.SemaphoreType.DMA((2, 4)),
        ],
        compiler_params=PARAMS,
        cost_estimate=cost(2.7),
        name="own_end",
    )(key_first, value_first, *in_hbm(key, value), rates)


def pair_kernel(own_ref, got_ref, tables_ref, pair_ref):
    _, _, _, odd = position()
    own, got = own_ref[...], got_ref[...]
    earlier, later = jnp.where(odd == 1, got, own), jnp.where(odd == 1, own, got)
    pair_ref[...] = tables_ref[0] * earlier + later


def row_kernel(own_ref, got_ref, tables_ref, row_ref):
    _, _, pair, _ = position()
    own, got = own_ref[...], got_ref[...]
    earlier, later = jnp.where(pair == 1, got, own), jnp.where(pair == 1, own, got)
    row_ref[...] = tables_ref[1] * earlier + later


def plane_kernel(own_ref, got_ref, tables_ref, plane_ref):
    plane_ref[...] = tables_ref[2] * own_ref[...] + tables_ref[3] * got_ref[...]


def states_kernel(own_ref, got_ref, pair_ref, half_ref, p1, p2, p3, tables_ref, mine_ref, other_ref):
    _, z, pair, odd = position()
    head = half_ref[...] * z.astype(F32) + add_up([tables_ref[3 + k] * p[...] for k, p in ((1, p1), (2, p2), (3, p3))])
    earlier = jnp.where(pair == 1, tables_ref[1] * head + pair_ref[...], head)
    later = tables_ref[0] * earlier + jnp.where(odd == 1, got_ref[...], own_ref[...])
    mine_ref[...] = jnp.where(odd == 1, later, earlier)
    other_ref[...] = jnp.where(odd == 1, earlier, later)


def small(kernel, count, *args):
    out = jax.ShapeDtypeStruct(args[0].shape, F32)
    return pl.pallas_call(
        kernel,
        in_specs=[IN_VMEM] * len(args),
        out_specs=[IN_VMEM] * count,
        out_shape=[out] * count,
        compiler_params=PARAMS,
        cost_estimate=cost(0.05),
        name=kernel.__name__,
    )(*args)


def local_kernel(by, sent_ref, ends_ref, gate_ref, rates_ref, residues_ref, skip_ref,
                 mixed_ref, gate_out, start_ref, reach_ref, enter_ref, decay_ref, gate_held, gate_f32, sems):
    tokens, width = mixed_ref.shape
    span = tokens // SUB
    place = lax.broadcasted_iota(jnp.int32, (SUB, LANES), 0).astype(F32)

    def copy(t):
        there = lanes_at(half_of(by) * width + t * LANES)
        return pltpu.make_async_copy(gate_ref.at[:, there], gate_held.at[t], sems.at[t])

    for t in range(width // LANES):
        copy(t).start()

    def tile(t, _):
        lanes = lanes_at(half_of(by) * width + t * LANES)
        here = lanes_at(t * LANES)
        rates = rates_ref[:, lanes]
        residues = residues_ref[:, lanes]
        decay = jnp.exp(-rates)
        decay_ref[:, here] = decay

        taps, term = [], residues
        for k in range(RUN):
            tap = term[:SUB] + term[SUB:]
            for shift in (4, 2, 1):
                tap = tap + pltpu.roll(tap, shift, 0)
            taps.append(tap)
            term = term * decay
        taps[0] = taps[0] + skip_ref[:, lanes]

        run = spread(jnp.exp(rates * float(-RUN)))

        def end(g, n):
            return ends_ref[pl.ds((g * ORDER + n) * SUB, SUB), here]

        state = [(end(0, n) * run[n] + end(1, n)) * run[n] + end(2, n) for n in range(ORDER)]
        for step in (1, 2, 4):
            across = spread(jnp.exp(rates * float(-span * step)))
            state = [s + later(s, step) * a for s, a in zip(state, across)]
        first = spread(residues * decay)
        for n in range(ORDER):
            rows = pl.ds(n * SUB, SUB)
            start_ref[rows, here] = first[n] * later(state[n], 1)
            reach_ref[rows, here] = first[n] * jnp.exp(rates[n : n + 1, :] * (place * float(-span)))
            for g in (0, 1):
                enter_ref[pl.ds((g * ORDER + n) * SUB, SUB), here] = first[n] * end(g, n)

        def group(g, _):
            signal = []
            for i in range(RUN):
                rows = pl.ds(pl.multiple_of((g * RUN + i) * SUB, SUB), SUB)
                signal.append(sent_ref[rows, here])
                mixed_ref[rows, here] = add_up([taps[i - m] * signal[m] for m in range(i + 1)])
            return 0

        lax.fori_loop(0, span // RUN, group, 0)
        return 0

    def gating(t, _):
        here = lanes_at(t * LANES)
        copy(t).wait()
        for s in range(SUB):
            gate_f32[pl.ds(s * PITCH, span), :] = gate_held[t, pl.ds(s * span, span), :].astype(F32)
        for j in range(span):
            rows = pl.ds(j * SUB, SUB)
            gate = gate_f32[pl.ds(j, SUB, stride=PITCH), :]
            mixed_ref[rows, here] = gate * mixed_ref[rows, here]
            gate_out[rows, here] = gate
        return 0

    lax.fori_loop(0, width // LANES, tile, 0)
    lax.fori_loop(0, width // LANES, gating, 0)


def local_part(by, sent, ends, gate, rates, residues, skip):
    tokens, width = sent.shape
    token_part = jax.ShapeDtypeStruct((tokens, width), F32)
    mode_part = jax.ShapeDtypeStruct((ORDER * SUB, width), F32)
    enter_part = jax.ShapeDtypeStruct((2 * ORDER * SUB, width), F32)
    decay_part = jax.ShapeDtypeStruct((ORDER, width), F32)
    gate = pltpu.with_memory_space_constraint(gate, pltpu.HBM)
    return pl.pallas_call(
        lambda *refs: local_kernel(by, *refs),
        in_specs=[IN_VMEM, IN_VMEM, IN_HBM, IN_VMEM, IN_VMEM, IN_VMEM],
        out_specs=[IN_VMEM] * 6,
        out_shape=[token_part, token_part, mode_part, mode_part, enter_part, decay_part],
        scratch_shapes=[
            pltpu.VMEM((width // LANES, tokens, LANES), BF16),
            pltpu.VMEM((SUB * PITCH, LANES), F32),
            pltpu.SemaphoreType.DMA((width // LANES,)),
        ],
        compiler_params=PARAMS,
        cost_estimate=cost(2.6),
        name="local_part",
    )(sent, ends, gate, rates, residues, skip)


def mix_kernel(by, last, mixed_ref, gate_ref, start_ref, reach_ref, enter_ref, decay_ref, state_ref, *rest):
    tokens, width = mixed_ref.shape
    span = tokens // SUB
    gated_ref, sums_ref = rest[-2], rest[-1]
    if by == 0:
        sums_ref[...] = jnp.zeros_like(sums_ref)
    else:
        sums_ref[...] = rest[0][...]
    if last:
        power_ref = rest[1]

    def tile(t, _):
        here = lanes_at(t * LANES)
        step = spread(decay_ref[:, here])
        state = state_ref[:, here]
        terms = []
        for n in range(ORDER):
            rows = pl.ds(n * SUB, SUB)
            terms.append(start_ref[rows, here] + reach_ref[rows, here] * state[n : n + 1, :])
        for j in range(span):
            if j > 0:
                terms = [a * b for a, b in zip(terms, step)]
            if j > 0 and j % RUN == 0:
                g = j // RUN - 1
                terms = [a + enter_ref[pl.ds((g * ORDER + n) * SUB, SUB), here] for n, a in enumerate(terms)]
            rows = pl.ds(j * SUB, SUB)
            gated = mixed_ref[rows, here] + gate_ref[rows, here] * add_up(terms)
            gated_ref[t, pl.ds(j, SUB, stride=OUT_PITCH), :] = gated
            sums_ref[rows, :] += gated * gated
        return 0

    lax.fori_loop(0, width // LANES, tile, 0)
    if last:
        for block in range(tokens // LANES):
            rows = pl.ds(block * LANES, LANES)
            power_ref[:, rows] = jnp.sum(jnp.transpose(sums_ref[rows, :]), axis=0, keepdims=True)


def mix(by, last, part, state, sums):
    tokens, width = part[0].shape
    out_sums = jax.ShapeDtypeStruct((tokens, LANES), F32)
    gated = jax.ShapeDtypeStruct((width // LANES, SUB * OUT_PITCH, LANES), F32)
    args = [*part, state] + ([] if sums is None else [sums])
    if last:
        outs, scratch = [jax.ShapeDtypeStruct((1, tokens), F32), gated], [pltpu.VMEM((tokens, LANES), F32)]
    else:
        outs, scratch = [gated, out_sums], []
    return pl.pallas_call(
        lambda *refs: mix_kernel(by, last, *refs),
        in_specs=[IN_VMEM] * len(args),
        out_specs=[IN_VMEM] * 2,
        out_shape=outs,
        scratch_shapes=scratch,
        compiler_params=PARAMS,
        cost_estimate=cost(2.1),
        name="mix",
    )(*args)


def norm_kernel(g0, g1, gain_ref, p0_ref, p1_ref, p2_ref, p3_ref, out_ref, runs_ref, scale_ref, held, sems):
    tiles, tokens = g0.shape[0], scale_ref.shape[0]
    width = tiles * LANES
    span = tokens // SUB
    total = (p0_ref[...] + p1_ref[...]) + (p2_ref[...] + p3_ref[...])
    power = jnp.transpose(jnp.broadcast_to(total, (LANES, tokens)))
    runs_ref[...] = lax.rsqrt(power * (1.0 / D) + 1e-6)
    for i in range(span):
        scale_ref[pl.ds(i, SUB, stride=span), :] = runs_ref[pl.ds(i * SUB, SUB), :]

    copies = []
    cuts = sems.shape[1]
    step = width // cuts
    for by, gated_ref in enumerate((g0, g1)):
        first = half_of(by) * width

        def tile(t, _):
            here = lanes_at(t * LANES)
            gain = gain_ref[:, lanes_at(first + t * LANES)]
            for s in range(SUB):
                rows = pl.ds(s * span, span)
                gated = gated_ref[t, pl.ds(s * OUT_PITCH, span), :]
                held[by, rows, here] = (gated * scale_ref[rows, :] * gain).astype(BF16)
            return 0

        for cut in range(cuts):
            lax.fori_loop(cut * tiles // cuts, (cut + 1) * tiles // cuts, tile, 0)
            copy = pltpu.make_async_copy(
                held.at[by, :, pl.ds(cut * step, step)],
                out_ref.at[:, pl.ds(pl.multiple_of(first + cut * step, step), step)],
                sems.at[by, cut],
            )
            copy.start()
            copies.append(copy)
    for copy in copies:
        copy.wait()


def norm(gated, gain, powers):
    tiles, tokens = gated[0].shape[0], powers[0].shape[1]
    width = tiles * LANES
    channels = width * OWNERS
    return pl.pallas_call(
        norm_kernel,
        in_specs=[IN_VMEM] * 7,
        out_specs=IN_HBM,
        out_shape=jax.ShapeDtypeStruct((tokens, channels), BF16),
        scratch_shapes=[
            pltpu.VMEM((tokens, LANES), F32),
            pltpu.VMEM((tokens, LANES), F32),
            pltpu.VMEM((OWNERS, tokens, width), BF16),
            pltpu.SemaphoreType.DMA((OWNERS, 8)),
        ],
        compiler_params=PARAMS,
        cost_estimate=cost(1.7),
        name="norm",
    )(*gated, gain, *powers)


def with_partner(x, by):
    return lax.ppermute(x, "seq", [(i, i ^ by) for i in range(32)])


def over_x(x, by):
    return lax.ppermute(x, "seq", [(i, (i + 8 * by) % 32) for i in range(32)])


def over_ch(x, by):
    return lax.ppermute(x, "ch", [(i, i ^ by) for i in range(4)])


def body(gate, key, value, rates, residues, skip_gain, norm_gain):
    skip = skip_gain[None, :]
    tie = lax.optimization_barrier

    far, far_sent, far_ends, *first = far_end(key, value, rates)
    far, rates0 = tie((far, rates))
    got = with_partner(far, 1)
    own, own_sent, own_ends, tables = own_end(*first, key, value, rates0)
    (pair,) = small(pair_kernel, 1, own, got, tables)

    pair, rates1 = tie((pair, rates))
    other_pair = with_partner(pair, 3)
    far_part = local_part(1, far_sent, far_ends, gate, rates1, residues, skip)
    other_pair, *far_part = tie((other_pair, *far_part))
    (row,) = small(row_kernel, 1, pair, other_pair, tables)

    row, rates2 = tie((row, rates))
    other_row = with_partner(row, 4)
    own_part = local_part(0, own_sent, own_ends, gate, rates2, residues, skip)
    other_row, *own_part = tie((other_row, *own_part))
    (plane,) = small(plane_kernel, 1, row, other_row, tables)

    planes = [over_x(plane, k) for k in (1, 2, 3)]
    mine, theirs = small(states_kernel, 2, own, got, other_pair, other_row, *planes, tables)

    theirs = with_partner(theirs, 1)
    own_gated, sums = mix(0, False, own_part, mine, None)
    power, far_gated = mix(1, True, far_part, theirs, sums)
    powers = [power] + [over_ch(power, k) for k in (1, 2, 3)]
    return norm([own_gated, far_gated], norm_gain[None, :], powers)


def solution(mesh):
    placed = (
        P("seq", "ch"),
        P("seq", "ch"),
        P("seq", "ch"),
        P(None, "ch"),
        P(None, "ch"),
        P("ch"),
        P("ch"),
    )
    return jax.shard_map(
        body, mesh=mesh, in_specs=placed, out_specs=P("seq", "ch"), check_vma=False
    )
```

```python
import jax
import jax.numpy as jnp
from jax import lax
from jax.experimental import pallas as pl
from jax.experimental.pallas import tpu as pltpu
from jax.sharding import PartitionSpec as P

D = 8192
ORDER = 16
LANES = 128
SUB = 8
RUN = 16
PITCH = 52
OUT_PITCH = 50
OWNERS = 2
F32 = jnp.float32
BF16 = jnp.bfloat16

IN_HBM = pl.BlockSpec(memory_space=pltpu.HBM)
IN_VMEM = pl.BlockSpec(memory_space=pltpu.VMEM)
PARAMS = pltpu.CompilerParams(vmem_limit_bytes=24 << 20)


def cost(us):
    return pl.CostEstimate(flops=int(us * 1.15e9), bytes_accessed=int(us * 3.69e6), transcendentals=0)


def spread(table):
    return [jnp.broadcast_to(table[n : n + 1, :], (SUB, LANES)) for n in range(ORDER)]


def add_up(terms):
    terms = list(terms)
    while len(terms) > 1:
        terms = [a + b for a, b in zip(terms[::2], terms[1::2])] + terms[len(terms) & ~1 :]
    return terms[0]


def position():
    place = lax.axis_index("seq")
    return lax.div(place, 8), lax.rem(lax.div(place, 4), 2), lax.rem(lax.div(place, 2), 2), lax.rem(place, 2)


def half_of(by):
    _, _, pair, odd = position()
    return lax.rem(pair + odd + by, 2)


def lanes_at(first):
    return pl.ds(pl.multiple_of(first, LANES), LANES)


def later(x, by):
    place = lax.broadcasted_iota(jnp.int32, (SUB, LANES), 0)
    return jnp.where(place >= by, pltpu.roll(x, by, 0), 0.0)


def fill_decays(span, rates_ref, first, decays_ref):
    def tile(t, _):
        rates = rates_ref[:, lanes_at(first + t * LANES)]
        for i, length in enumerate((1, RUN, span, 2 * span, 4 * span)):
            decays_ref[i, :, lanes_at(t * LANES)] = jnp.exp(rates * float(-length))
        return 0

    lax.fori_loop(0, decays_ref.shape[2] // LANES, tile, 0)


def end_of_tile(span, signal_ref, decays_ref, sent_ref, ends_ref, here):
    one = spread(decays_ref[0, :, here])
    run = spread(decays_ref[1, :, here])
    total = None
    for g in range(span // RUN):
        acc = None
        for i in range(RUN):
            j = g * RUN + i
            signal = signal_ref[pl.ds(j, SUB, stride=PITCH), :]
            sent_ref[pl.ds(j * SUB, SUB), here] = signal
            acc = [signal] * ORDER if acc is None else [a * o + signal for a, o in zip(acc, one)]
        for n in range(ORDER):
            ends_ref[pl.ds((g * ORDER + n) * SUB, SUB), here] = acc[n]
        total = acc if total is None else [t * r + a for t, r, a in zip(total, run, acc)]
    for i, by in enumerate((1, 2, 4)):
        across = spread(decays_ref[2 + i, :, here])
        total = [t + pltpu.roll(t, by, 0) * a for t, a in zip(total, across)]
    return [t[SUB - 1 :, :] for t in total]


def end_of_piece(key_ref, value_ref, decays_ref, signal_ref, sent_ref, ends_ref, end_ref, at):
    span = key_ref.shape[0] // SUB

    def tile(t, _):
        there, here = lanes_at(t * LANES), lanes_at(at + t * LANES)
        for s in range(SUB):
            rows = pl.ds(s * span, span)
            signal_ref[pl.ds(s * PITCH, span), :] = key_ref[rows, there].astype(F32) * value_ref[rows, there].astype(F32)
        ends = end_of_tile(span, signal_ref, decays_ref, sent_ref, ends_ref, here)
        for n in range(ORDER):
            end_ref[n : n + 1, here] = ends[n]
        return 0

    lax.fori_loop(0, key_ref.shape[1] // LANES, tile, 0, unroll=2)


def half_copies(by, sources, targets, sems, cuts, which):
    width = sources[0].shape[1] // OWNERS
    step = width // cuts
    return [
        [
            pltpu.make_async_copy(
                a.at[:, pl.ds(pl.multiple_of(half_of(by) * width + j * step, step), step)],
                b.at[:, pl.ds(j * step, step)],
                sems.at[s, j],
            )
            for s, (a, b) in enumerate(zip(sources, targets))
        ]
        for j in which
    ]


def far_end_kernel(key_ref, value_ref, rates_ref, end_ref, sent_ref, ends_ref, key_own, value_own,
                   key_held, value_held, signal_ref, rates_here, decays_ref, sems, sem):
    width = key_held.shape[1]
    cuts = 4
    step = width // cuts
    sources = (key_ref, value_ref)
    pieces = half_copies(1, sources, (key_held, value_held), sems.at[0], cuts, range(cuts))
    pieces += half_copies(0, sources, (key_own, value_own), sems.at[1], cuts, range(key_own.shape[1] // step))
    rates_copy = pltpu.make_async_copy(rates_ref, rates_here, sem)
    rates_copy.start()
    ahead = 3
    for i in range(ahead):
        for c in pieces[i]:
            c.start()
    rates_copy.wait()
    fill_decays(key_ref.shape[0] // SUB, rates_here, half_of(1) * width, decays_ref)
    for i in range(cuts):
        for c in pieces[i]:
            c.wait()
        if i + ahead < len(pieces):
            for c in pieces[i + ahead]:
                c.start()
        part = pl.ds(i * step, step)
        end_of_piece(key_held.at[:, part], value_held.at[:, part], decays_ref,
                     signal_ref, sent_ref, ends_ref, end_ref, i * step)
    for p in pieces[cuts:]:
        for c in p:
            c.wait()


def end_shapes(tokens, width):
    part = jax.ShapeDtypeStruct((tokens, width), F32)
    return [jax.ShapeDtypeStruct((ORDER, width), F32), part, part]


def in_hbm(*arrays):
    return [pltpu.with_memory_space_constraint(a, pltpu.HBM) for a in arrays]


def far_end(key, value, rates):
    tokens, channels = key.shape
    width = channels // OWNERS
    return pl.pallas_call(
        far_end_kernel,
        in_specs=[IN_HBM] * 3,
        out_specs=[IN_VMEM] * 5,
        out_shape=end_shapes(tokens, width) + [jax.ShapeDtypeStruct((tokens, width // 2), BF16)] * 2,
        scratch_shapes=[
            pltpu.VMEM((tokens, width), BF16),
            pltpu.VMEM((tokens, width), BF16),
            pltpu.VMEM((SUB * PITCH, LANES), F32),
            pltpu.VMEM((ORDER, channels), F32),
            pltpu.VMEM((5, ORDER, width), F32),
            pltpu.SemaphoreType.DMA((2, 2, 4)),
            pltpu.SemaphoreType.DMA(()),
        ],
        compiler_params=PARAMS,
        cost_estimate=cost(3.4),
        name="far_end",
    )(*in_hbm(key, value, rates))


ENTRIES = 7


def own_end_kernel(key_first, value_first, key_ref, value_ref, rates_ref, end_ref, sent_ref, ends_ref, tables_ref,
                   key_held, value_held, signal_ref, decays_ref, sems):
    tokens, width = key_held.shape
    x, z, _, _ = position()
    first = half_of(0) * width
    cuts = 4
    step = width // cuts
    brought = key_first.shape[1] // step
    pieces = half_copies(0, (key_ref, value_ref), (key_held, value_held), sems, cuts, range(brought, cuts))
    for p in pieces:
        for c in p:
            c.start()

    def table(t, _):
        here = lanes_at(t * LANES)
        rates = rates_ref[:, lanes_at(first + t * LANES)] * float(-tokens)
        tables_ref[0, :, here] = jnp.exp(rates)
        tables_ref[1, :, here] = jnp.exp(rates * 2.0)
        tables_ref[2, :, here] = jnp.exp(rates * (4 * (1 - z)).astype(F32))
        tables_ref[3, :, here] = jnp.exp(rates * (4 * z).astype(F32))
        for k in (1, 2, 3):
            spans = (4 * z + 8 * (k - 1)).astype(F32)
            tables_ref[3 + k, :, here] = jnp.exp(rates * spans) * (x >= k).astype(F32)
        return 0

    lax.fori_loop(0, width // LANES, table, 0)
    fill_decays(tokens // SUB, rates_ref, first, decays_ref)
    for i in range(cuts):
        part = pl.ds(i * step, step)
        if i < brought:
            key, value = key_first, value_first
        else:
            key, value = key_held, value_held
            for c in pieces[i - brought]:
                c.wait()
        end_of_piece(key.at[:, part], value.at[:, part], decays_ref,
                     signal_ref, sent_ref, ends_ref, end_ref, i * step)


def own_end(key_first, value_first, key, value, rates):
    tokens, channels = key.shape
    width = channels // OWNERS
    return pl.pallas_call(
        own_end_kernel,
        in_specs=[IN_VMEM, IN_VMEM, IN_HBM, IN_HBM, IN_VMEM],
        out_specs=[IN_VMEM] * 4,
        out_shape=end_shapes(tokens, width) + [jax.ShapeDtypeStruct((ENTRIES, ORDER, width), F32)],
        scratch_shapes=[
            pltpu.VMEM((tokens, width), BF16),
            pltpu.VMEM((tokens, width), BF16),
            pltpu.VMEM((SUB * PITCH, LANES), F32),
            pltpu.VMEM((5, ORDER, width), F32),
            pltpu.SemaphoreType.DMA((2, 4)),
        ],
        compiler_params=PARAMS,
        cost_estimate=cost(2.7),
        name="own_end",
    )(key_first, value_first, *in_hbm(key, value), rates)


def pair_kernel(own_ref, got_ref, tables_ref, pair_ref):
    _, _, _, odd = position()
    own, got = own_ref[...], got_ref[...]
    earlier, later = jnp.where(odd == 1, got, own), jnp.where(odd == 1, own, got)
    pair_ref[...] = tables_ref[0] * earlier + later


def row_kernel(own_ref, got_ref, tables_ref, row_ref):
    _, _, pair, _ = position()
    own, got = own_ref[...], got_ref[...]
    earlier, later = jnp.where(pair == 1, got, own), jnp.where(pair == 1, own, got)
    row_ref[...] = tables_ref[1] * earlier + later


def plane_kernel(own_ref, got_ref, tables_ref, plane_ref):
    plane_ref[...] = tables_ref[2] * own_ref[...] + tables_ref[3] * got_ref[...]


def states_kernel(own_ref, got_ref, pair_ref, half_ref, p1, p2, p3, tables_ref, mine_ref, other_ref):
    _, z, pair, odd = position()
    head = half_ref[...] * z.astype(F32) + add_up([tables_ref[3 + k] * p[...] for k, p in ((1, p1), (2, p2), (3, p3))])
    earlier = jnp.where(pair == 1, tables_ref[1] * head + pair_ref[...], head)
    later = tables_ref[0] * earlier + jnp.where(odd == 1, got_ref[...], own_ref[...])
    mine_ref[...] = jnp.where(odd == 1, later, earlier)
    other_ref[...] = jnp.where(odd == 1, earlier, later)


def small(kernel, count, *args):
    out = jax.ShapeDtypeStruct(args[0].shape, F32)
    return pl.pallas_call(
        kernel,
        in_specs=[IN_VMEM] * len(args),
        out_specs=[IN_VMEM] * count,
        out_shape=[out] * count,
        compiler_params=PARAMS,
        cost_estimate=cost(0.05),
        name=kernel.__name__,
    )(*args)


def local_kernel(by, sent_ref, ends_ref, gate_ref, rates_ref, residues_ref, skip_ref,
                 mixed_ref, gate_out, start_ref, reach_ref, enter_ref, decay_ref, gate_held, gate_f32, sems):
    tokens, width = mixed_ref.shape
    span = tokens // SUB
    place = lax.broadcasted_iota(jnp.int32, (SUB, LANES), 0).astype(F32)

    def copy(t):
        there = lanes_at(half_of(by) * width + t * LANES)
        return pltpu.make_async_copy(gate_ref.at[:, there], gate_held.at[t], sems.at[t])

    for t in range(width // LANES):
        copy(t).start()

    def tile(t, _):
        lanes = lanes_at(half_of(by) * width + t * LANES)
        here = lanes_at(t * LANES)
        rates = rates_ref[:, lanes]
        residues = residues_ref[:, lanes]
        decay = jnp.exp(-rates)
        decay_ref[:, here] = decay

        taps, term = [], residues
        for k in range(RUN):
            tap = term[:SUB] + term[SUB:]
            for shift in (4, 2, 1):
                tap = tap + pltpu.roll(tap, shift, 0)
            taps.append(tap)
            term = term * decay
        taps[0] = taps[0] + skip_ref[:, lanes]

        run = spread(jnp.exp(rates * float(-RUN)))

        def end(g, n):
            return ends_ref[pl.ds((g * ORDER + n) * SUB, SUB), here]

        state = [(end(0, n) * run[n] + end(1, n)) * run[n] + end(2, n) for n in range(ORDER)]
        for step in (1, 2, 4):
            across = spread(jnp.exp(rates * float(-span * step)))
            state = [s + later(s, step) * a for s, a in zip(state, across)]
        first = spread(residues * decay)
        for n in range(ORDER):
            rows = pl.ds(n * SUB, SUB)
            start_ref[rows, here] = first[n] * later(state[n], 1)
            reach_ref[rows, here] = first[n] * jnp.exp(rates[n : n + 1, :] * (place * float(-span)))
            for g in (0, 1):
                enter_ref[pl.ds((g * ORDER + n) * SUB, SUB), here] = first[n] * end(g, n)

        def group(g, _):
            signal = []
            for i in range(RUN):
                rows = pl.ds(pl.multiple_of((g * RUN + i) * SUB, SUB), SUB)
                signal.append(sent_ref[rows, here])
                mixed_ref[rows, here] = add_up([taps[i - m] * signal[m] for m in range(i + 1)])
            return 0

        lax.fori_loop(0, span // RUN, group, 0)
        return 0

    def gating(t, _):
        here = lanes_at(t * LANES)
        copy(t).wait()
        for s in range(SUB):
            gate_f32[pl.ds(s * PITCH, span), :] = gate_held[t, pl.ds(s * span, span), :].astype(F32)
        for j in range(span):
            rows = pl.ds(j * SUB, SUB)
            gate = gate_f32[pl.ds(j, SUB, stride=PITCH), :]
            mixed_ref[rows, here] = gate * mixed_ref[rows, here]
            gate_out[rows, here] = gate
        return 0

    lax.fori_loop(0, width // LANES, tile, 0)
    lax.fori_loop(0, width // LANES, gating, 0)


def local_part(by, sent, ends, gate, rates, residues, skip):
    tokens, width = sent.shape
    token_part = jax.ShapeDtypeStruct((tokens, width), F32)
    mode_part = jax.ShapeDtypeStruct((ORDER * SUB, width), F32)
    enter_part = jax.ShapeDtypeStruct((2 * ORDER * SUB, width), F32)
    decay_part = jax.ShapeDtypeStruct((ORDER, width), F32)
    gate = pltpu.with_memory_space_constraint(gate, pltpu.HBM)
    return pl.pallas_call(
        lambda *refs: local_kernel(by, *refs),
        in_specs=[IN_VMEM, IN_VMEM, IN_HBM, IN_VMEM, IN_VMEM, IN_VMEM],
        out_specs=[IN_VMEM] * 6,
        out_shape=[token_part, token_part, mode_part, mode_part, enter_part, decay_part],
        scratch_shapes=[
            pltpu.VMEM((width // LANES, tokens, LANES), BF16),
            pltpu.VMEM((SUB * PITCH, LANES), F32),
            pltpu.SemaphoreType.DMA((width // LANES,)),
        ],
        compiler_params=PARAMS,
        cost_estimate=cost(2.6),
        name="local_part",
    )(sent, ends, gate, rates, residues, skip)


def mix_kernel(by, last, mixed_ref, gate_ref, start_ref, reach_ref, enter_ref, decay_ref, state_ref, *rest):
    tokens, width = mixed_ref.shape
    span = tokens // SUB
    gated_ref, sums_ref = rest[-2], rest[-1]
    if by == 0:
        sums_ref[...] = jnp.zeros_like(sums_ref)
    else:
        sums_ref[...] = rest[0][...]
    if last:
        power_ref = rest[1]

    def tile(t, _):
        here = lanes_at(t * LANES)
        step = spread(decay_ref[:, here])
        state = state_ref[:, here]
        terms = []
        for n in range(ORDER):
            rows = pl.ds(n * SUB, SUB)
            terms.append(start_ref[rows, here] + reach_ref[rows, here] * state[n : n + 1, :])
        for j in range(span):
            if j > 0:
                terms = [a * b for a, b in zip(terms, step)]
            if j > 0 and j % RUN == 0:
                g = j // RUN - 1
                terms = [a + enter_ref[pl.ds((g * ORDER + n) * SUB, SUB), here] for n, a in enumerate(terms)]
            rows = pl.ds(j * SUB, SUB)
            gated = mixed_ref[rows, here] + gate_ref[rows, here] * add_up(terms)
            gated_ref[t, pl.ds(j, SUB, stride=OUT_PITCH), :] = gated
            sums_ref[rows, :] += gated * gated
        return 0

    lax.fori_loop(0, width // LANES, tile, 0, unroll=2)
    if last:
        for block in range(tokens // LANES):
            rows = pl.ds(block * LANES, LANES)
            power_ref[:, rows] = jnp.sum(jnp.transpose(sums_ref[rows, :]), axis=0, keepdims=True)


def mix(by, last, part, state, sums):
    tokens, width = part[0].shape
    out_sums = jax.ShapeDtypeStruct((tokens, LANES), F32)
    gated = jax.ShapeDtypeStruct((width // LANES, SUB * OUT_PITCH, LANES), F32)
    args = [*part, state] + ([] if sums is None else [sums])
    if last:
        outs, scratch = [jax.ShapeDtypeStruct((1, tokens), F32), gated], [pltpu.VMEM((tokens, LANES), F32)]
    else:
        outs, scratch = [gated, out_sums], []
    return pl.pallas_call(
        lambda *refs: mix_kernel(by, last, *refs),
        in_specs=[IN_VMEM] * len(args),
        out_specs=[IN_VMEM] * 2,
        out_shape=outs,
        scratch_shapes=scratch,
        compiler_params=PARAMS,
        cost_estimate=cost(2.1),
        name="mix",
    )(*args)


def norm_kernel(g0, g1, gain_ref, p0_ref, p1_ref, p2_ref, p3_ref, out_ref, runs_ref, scale_ref, held, sems):
    tiles, tokens = g0.shape[0], scale_ref.shape[0]
    width = tiles * LANES
    span = tokens // SUB
    total = (p0_ref[...] + p1_ref[...]) + (p2_ref[...] + p3_ref[...])
    power = jnp.transpose(jnp.broadcast_to(total, (LANES, tokens)))
    runs_ref[...] = lax.rsqrt(power * (1.0 / D) + 1e-6)
    for i in range(span):
        scale_ref[pl.ds(i, SUB, stride=span), :] = runs_ref[pl.ds(i * SUB, SUB), :]

    copies = []
    cuts = sems.shape[1]
    step = width // cuts
    for by, gated_ref in enumerate((g0, g1)):
        first = half_of(by) * width

        def tile(t, _):
            here = lanes_at(t * LANES)
            gain = gain_ref[:, lanes_at(first + t * LANES)]
            for s in range(SUB):
                rows = pl.ds(s * span, span)
                gated = gated_ref[t, pl.ds(s * OUT_PITCH, span), :]
                held[by, rows, here] = (gated * scale_ref[rows, :] * gain).astype(BF16)
            return 0

        for cut in range(cuts):
            lax.fori_loop(cut * tiles // cuts, (cut + 1) * tiles // cuts, tile, 0)
            copy = pltpu.make_async_copy(
                held.at[by, :, pl.ds(cut * step, step)],
                out_ref.at[:, pl.ds(pl.multiple_of(first + cut * step, step), step)],
                sems.at[by, cut],
            )
            copy.start()
            copies.append(copy)
    for copy in copies:
        copy.wait()


def norm(gated, gain, powers):
    tiles, tokens = gated[0].shape[0], powers[0].shape[1]
    width = tiles * LANES
    channels = width * OWNERS
    return pl.pallas_call(
        norm_kernel,
        in_specs=[IN_VMEM] * 7,
        out_specs=IN_HBM,
        out_shape=jax.ShapeDtypeStruct((tokens, channels), BF16),
        scratch_shapes=[
            pltpu.VMEM((tokens, LANES), F32),
            pltpu.VMEM((tokens, LANES), F32),
            pltpu.VMEM((OWNERS, tokens, width), BF16),
            pltpu.SemaphoreType.DMA((OWNERS, 8)),
        ],
        compiler_params=PARAMS,
        cost_estimate=cost(1.7),
        name="norm",
    )(*gated, gain, *powers)


def with_partner(x, by):
    return lax.ppermute(x, "seq", [(i, i ^ by) for i in range(32)])


def over_x(x, by):
    return lax.ppermute(x, "seq", [(i, (i + 8 * by) % 32) for i in range(32)])


def over_ch(x, by):
    return lax.ppermute(x, "ch", [(i, i ^ by) for i in range(4)])


def body(gate, key, value, rates, residues, skip_gain, norm_gain):
    skip = skip_gain[None, :]
    tie = lax.optimization_barrier

    far, far_sent, far_ends, *first = far_end(key, value, rates)
    far, rates0 = tie((far, rates))
    got = with_partner(far, 1)
    own, own_sent, own_ends, tables = own_end(*first, key, value, rates0)
    (pair,) = small(pair_kernel, 1, own, got, tables)

    pair, rates1 = tie((pair, rates))
    other_pair = with_partner(pair, 3)
    far_part = local_part(1, far_sent, far_ends, gate, rates1, residues, skip)
    other_pair, *far_part = tie((other_pair, *far_part))
    (row,) = small(row_kernel, 1, pair, other_pair, tables)

    row, rates2 = tie((row, rates))
    other_row = with_partner(row, 4)
    own_part = local_part(0, own_sent, own_ends, gate, rates2, residues, skip)
    other_row, *own_part = tie((other_row, *own_part))
    (plane,) = small(plane_kernel, 1, row, other_row, tables)

    planes = [over_x(plane, k) for k in (1, 2, 3)]
    mine, theirs = small(states_kernel, 2, own, got, other_pair, other_row, *planes, tables)

    theirs = with_partner(theirs, 1)
    own_gated, sums = mix(0, False, own_part, mine, None)
    power, far_gated = mix(1, True, far_part, theirs, sums)
    powers = [power] + [over_ch(power, k) for k in (1, 2, 3)]
    return norm([own_gated, far_gated], norm_gain[None, :], powers)


def solution(mesh):
    placed = (
        P("seq", "ch"),
        P("seq", "ch"),
        P("seq", "ch"),
        P(None, "ch"),
        P(None, "ch"),
        P("ch"),
        P("ch"),
    )
    return jax.shard_map(
        body, mesh=mesh, in_specs=placed, out_specs=P("seq", "ch"), check_vma=False
    )
```
